32 devices in a mesh: tile: 8 (over z, x), owner: 4 (over y, core).
Axes of the slice: x: 2, y: 2, z: 4, core: 2. Of those that a mesh axis runs over, the one named last changes fastest.
Arguments:
- potential: bfloat16 [2, 8, 1024, 256], P(None, 'tile', 'owner'), may hold values from -6 to 6
- positions: int32 [128, 2], P(('tile', 'owner')), may hold values from 0 to 1792, as said below
- illumination: float32 [2, 256, 256], replicated, may hold values from -5 to 5
- measured: float32 [128, 256, 256], P(('tile', 'owner')), may hold values from 0 to 2
Outputs:
- gradient: float32 [2, 8, 1024, 256], P(None, 'tile', 'owner')
The draws below stay inside these ranges and needn't reach their ends.
Inputs may be any that keep to these rules, and one draw needn't show every extreme that they name: `positions`: probe p belongs to tile p // 16: its window starts inside that tile and lies inside the object grid, reaching at most into the tiles to the right, below and below-right.
All inputs are finite; a program needn't handle non-finite values.
Results may differ from the reference program's by a relative error of at most 0.0003.
Values may be sent and summed in bfloat16 or wider, within the bound.
A program may use at most 64 MiB of HBM per device.

```python
import math
import jax
import jax.numpy as jnp
from jax import lax

SLICES = 2
PW = 256
TH = 1024
TW = 256
TX = 8
TILES = 8
GROUP = 16
PROBES = 128


def draw_positions(key, part):
    indices = jnp.arange(PROBES, dtype=jnp.int32)
    tile_id = indices // GROUP
    tile_row = tile_id // TX
    tile_col = tile_id % TX
    row_limit = jnp.where(tile_row == TILES // TX - 1, TH - PW + 1, TH)
    col_limit = jnp.where(tile_col == TX - 1, TW - PW + 1, TW)
    row_key, col_key = jax.random.split(jax.random.fold_in(key, 11))
    row_draw = jax.random.randint(row_key, (PROBES,), 0, 1 << 30, dtype=jnp.int32) % row_limit
    col_draw = jax.random.randint(col_key, (PROBES,), 0, 1 << 30, dtype=jnp.int32) % col_limit
    member = indices % GROUP
    row_offset = jnp.where(member == 0, row_limit - 1, jnp.where(member == 1, 0, row_draw))
    col_offset = jnp.where(member == 0, col_limit - 1, jnp.where(member == 1, 0, col_draw))
    return jnp.stack([tile_row * TH + row_offset, tile_col * TW + col_offset], axis=1).astype(jnp.int32)


def shard_levels(stream_key, shape, cuts, least, top_value):
    level, own = 1.0, jax.random.fold_in(stream_key, 6)
    for dim, parts in cuts:
        steps = jnp.exp(jax.random.uniform(jax.random.fold_in(own, dim), (parts,), jnp.float32, least / len(cuts), top_value / len(cuts)))
        level = level * jnp.repeat(steps, shape[dim] // parts).reshape([-1 if axis == dim else 1 for axis in range(len(shape))])
    return level


def normal_values(rng, shape, width, limit, shards=(), kind=jnp.bfloat16):
    values = jax.random.normal(rng, shape, jnp.float32) * width
    if len(shards) > 0:
        values = shard_levels(rng, shape, shards, -0.22, 0.18) * values
    return jnp.clip(values, min=-limit, max=limit).astype(kind)


def setup_inputs(seed: int = 0) -> dict:
    keys = jax.random.split(jax.random.key(seed), 5)
    potential = normal_values(keys[0], (SLICES, TILES, TH, TW), 1.0, 6.0, ((1, 8), (2, 4)))
    positions = draw_positions(jax.random.fold_in(keys[4], 71), 0)
    illumination = normal_values(keys[2], (2, PW, PW), 0.7, 5.0, (), jnp.float32)
    measured = jnp.clip(2.0 * jax.random.uniform(keys[3], (PROBES, PW, PW), jnp.float32) ** shard_levels(keys[3], (PROBES, PW, PW), ((0, 32),), -0.2, 0.2), 0.0, 2.0)
    return {"potential": potential, "positions": positions, "illumination": illumination, "measured": measured}


SIGMA = 0.5
LOSS_WEIGHT = 0.125

def probe_loss(window_cut, illumination, measured):
    probe_width = illumination.shape[1]
    counter = jnp.arange(probe_width, dtype=jnp.int32)
    signed = (counter + probe_width // 2) % probe_width - probe_width // 2
    square = (signed * signed).astype(jnp.float32)
    phase_angle = 4.0 * math.pi / (probe_width * probe_width) * (square[:, None] + square[None, :])
    transfer = lax.complex(jnp.cos(phase_angle), -jnp.sin(phase_angle))
    wave = lax.complex(illumination[0], illumination[1])
    layers = window_cut.shape[0]
    for layer_index in range(layers):
        turn = SIGMA * window_cut[layer_index]
        wave = wave * lax.complex(jnp.cos(turn), jnp.sin(turn))
        if layer_index + 1 < layers:
            wave = jnp.fft.ifft2(jnp.fft.fft2(wave, norm='ortho') * transfer, norm='ortho')
    far_field = jnp.fft.fft2(wave, norm='ortho')
    far_real = jnp.real(far_field)
    far_imag = jnp.imag(far_field)
    misfit = far_real * far_real + far_imag * far_imag - measured
    return LOSS_WEIGHT * jnp.sum(misfit * misfit)

def reference(potential, positions, illumination, measured):
    tile_count = TILES // TX
    object_grid = potential.astype(jnp.float32).reshape(SLICES, tile_count, TX, TH, TW)
    object_grid = object_grid.transpose(0, 1, 3, 2, 4).reshape(SLICES, tile_count * TH, TX * TW)
    grad_fn = jax.grad(probe_loss)
    anchor = jnp.zeros((), jnp.int32)

    def probe_step(running, probe_item):
        position, target = probe_item
        corner = (anchor, position[0].astype(jnp.int32), position[1].astype(jnp.int32))
        window_cut = lax.dynamic_slice(object_grid, corner, (SLICES, PW, PW))
        local_grad = grad_fn(window_cut, illumination, target)
        current = lax.dynamic_slice(running, corner, (SLICES, PW, PW))
        return (lax.dynamic_update_slice(running, current + local_grad, corner), None)
    start = jnp.zeros(object_grid.shape, jnp.float32)
    running, _ = lax.scan(probe_step, start, (positions, measured))
    running = running.reshape(SLICES, tile_count, TH, TX, TW).transpose(0, 1, 3, 2, 4)
    return running.reshape(SLICES, TILES, TH, TW)
```

```python
import functools
import math

import jax
import jax.numpy as jnp
import numpy as np
from jax import lax
from jax.experimental import pallas as pl
from jax.experimental.pallas import tpu as pltpu
from jax.sharding import PartitionSpec as P

TX = 8

SIGMA = 0.5
LOSS_WEIGHT = 0.125
ALIGN = 16


def passed_along(block, axis, distance):
    devices = range(lax.axis_size(axis))
    route = [(i - distance, i) for i in devices if i - distance in devices]
    return lax.ppermute(block, axis, route)


def block_tables(width):
    counter = np.arange(width)
    signed = (counter + width // 2) % width - width // 2
    angle = 2.0 * np.pi / width * (counter[:, None] * counter[None, :] % width)
    dft = np.exp(-1j * angle) / math.sqrt(width)
    chirp = np.exp(-4j * np.pi * signed.astype(np.float64) ** 2 / (width * width))
    prop = (np.conj(dft) * chirp[None, :]) @ dft

    def right(m):
        return np.block([[m.real, m.imag], [-m.imag, m.real]])

    full = np.stack([right(dft), right(np.conj(dft)), right(prop), right(np.conj(prop))])
    full = full.astype(np.float32)
    high = full.astype(jnp.bfloat16)
    low = (full - high.astype(np.float32)).astype(jnp.bfloat16)
    return high, low


def halves(x):
    high = x.astype(jnp.bfloat16)
    low = (x - high.astype(jnp.float32)).astype(jnp.bfloat16)
    return high, low


def dot3(a, b):
    def dot(x, y):
        return jnp.dot(x, y, preferred_element_type=jnp.float32)

    return dot(a[0], b[0]) + (dot(a[0], b[1]) + dot(a[1], b[0]))


def both_sides(real, imag, high, low, which):
    width = real.shape[0]
    wide = jnp.concatenate([real, imag], axis=1)
    wide = dot3(halves(wide), (high[which], low[which]))
    tall = jnp.concatenate([wide[:, :width], wide[:, width:]], axis=0)
    other = which ^ 1
    tall = dot3((high[other], low[other]), halves(tall))
    return tall[:width], tall[width:]


def turn(window):
    y = (0.5 * SIGMA) * window
    z = y * y
    sine = -1.0 / 39916800.0
    for c in (1.0 / 362880.0, -1.0 / 5040.0, 1.0 / 120.0, -1.0 / 6.0, 1.0):
        sine = sine * z + c
    sine = sine * y
    cosine = 1.0 / 479001600.0
    for c in (-1.0 / 3628800.0, 1.0 / 40320.0, -1.0 / 720.0, 1.0 / 24.0, -0.5, 1.0):
        cosine = cosine * z + c
    return 1.0 - 2.0 * sine * sine, 2.0 * sine * cosine


def probes_kernel(corner_ref, ext_ref, illum_ref, meas_ref, high, low, acc_ref):
    width = illum_ref.shape[1]
    rows, cols = ext_ref.shape[1], ext_ref.shape[2]
    span = width + ALIGN
    acc_ref[...] = jnp.zeros_like(acc_ref)

    def probe(p, carry):
        r = corner_ref[p, 0]
        c = corner_ref[p, 1]
        base = pl.multiple_of(jnp.minimum((r // ALIGN) * ALIGN, rows - span), ALIGN)
        shift = r - base

        def cut(s):
            x = ext_ref[s, pl.ds(base, span), :].astype(jnp.float32)
            x = pltpu.roll(x, span - shift, 0)[:width]
            return pltpu.roll(x, cols - c, 1)[:, :width]

        def paste(s, g):
            x = jnp.concatenate([g, jnp.zeros((width, cols - width), jnp.float32)], axis=1)
            x = pltpu.roll(x, c, 1)
            x = jnp.concatenate([x, jnp.zeros((ALIGN, cols), jnp.float32)], axis=0)
            acc_ref[s, pl.ds(base, span), :] += pltpu.roll(x, shift, 0)

        cos0, sin0 = turn(cut(0))
        first_r = illum_ref[0] * cos0 - illum_ref[1] * sin0
        first_i = illum_ref[0] * sin0 + illum_ref[1] * cos0
        mid_r, mid_i = both_sides(first_r, first_i, high, low, 2)
        cos1, sin1 = turn(cut(1))
        exit_r = mid_r * cos1 - mid_i * sin1
        exit_i = mid_r * sin1 + mid_i * cos1
        far_r, far_i = both_sides(exit_r, exit_i, high, low, 0)
        misfit = far_r * far_r + far_i * far_i - meas_ref[p]
        scale = (4.0 * LOSS_WEIGHT) * misfit
        g_r, g_i = both_sides(scale * far_r, scale * far_i, high, low, 1)
        paste(1, SIGMA * (g_i * exit_r - g_r * exit_i))
        b_r = g_r * cos1 + g_i * sin1
        b_i = g_i * cos1 - g_r * sin1
        g_r, g_i = both_sides(b_r, b_i, high, low, 3)
        paste(0, SIGMA * (g_i * first_r - g_r * first_i))
        return carry

    lax.fori_loop(0, meas_ref.shape[0], probe, 0)


def probe_gradients(corners, extended, illumination, measured, interpret=False):
    high, low = block_tables(illumination.shape[1])
    vmem = pl.BlockSpec(memory_space=pltpu.VMEM)
    probes, width = measured.shape[0], measured.shape[1]
    flops = probes * 4 * 2 * 3 * 2 * (2 * width) ** 2 * width
    return pl.pallas_call(
        probes_kernel,
        out_shape=jax.ShapeDtypeStruct(extended.shape, jnp.float32),
        in_specs=[pl.BlockSpec(memory_space=pltpu.SMEM)] + [vmem] * 5,
        out_specs=vmem,
        compiler_params=pltpu.CompilerParams(vmem_limit_bytes=56 * 2**20),
        cost_estimate=pl.CostEstimate(flops=flops, bytes_accessed=16 * 2**20, transcendentals=0),
        interpret=interpret,
    )(corners, extended, illumination, measured, jnp.asarray(high), jnp.asarray(low))


def body(potential, positions, illumination, measured):
    probe_width = illumination.shape[1]
    rows_part = potential[:, 0]
    tile_rows = rows_part.shape[1] * lax.axis_size("owner")
    tile_cols = rows_part.shape[2]
    below = lax.axis_size("tile") > TX
    right_rim = passed_along(rows_part, "tile", -1)
    extended = lax.all_gather(
        jnp.concatenate([rows_part, right_rim], axis=2), "owner", axis=1, tiled=True
    )
    if below:
        lower_rim = passed_along(extended[:, :probe_width, :], "tile", -TX)
        extended = jnp.concatenate([extended, lower_rim], axis=1)
    tile_id = lax.axis_index("tile")
    first = jnp.stack([tile_id // TX * tile_rows, tile_id % TX * tile_cols])
    corners = positions - first[None, :].astype(jnp.int32)
    accumulated = probe_gradients(corners, extended, illumination, measured)
    wide_grad = accumulated[:, :tile_rows, :]
    if below:
        upper_back = passed_along(accumulated[:, tile_rows:, :], "tile", TX)
        wide_grad = wide_grad.at[:, :probe_width, :].add(upper_back)
    row_shard = lax.psum_scatter(wide_grad, "owner", scatter_dimension=1, tiled=True)
    left_back = passed_along(row_shard[:, :, tile_cols:], "tile", 1)
    result = row_shard[:, :, :tile_cols] + left_back
    return result[:, None]


def solution(mesh):
    in_specs = (
        P(None, "tile", "owner", None),
        P(("tile", "owner"), None),
        P(),
        P(("tile", "owner"), None, None),
    )
    out_specs = P(None, "tile", "owner", None)
    return jax.shard_map(body, mesh=mesh, in_specs=in_specs, out_specs=out_specs, check_vma=False)
```

```python
import functools
import math

import jax
import jax.numpy as jnp
import numpy as np
from jax import lax
from jax.experimental import pallas as pl
from jax.experimental.pallas import tpu as pltpu
from jax.sharding import PartitionSpec as P

TX = 8

SIGMA = 0.5
LOSS_WEIGHT = 0.125
ALIGN = 16
MESH = pl.DeviceIdType.MESH


def passed_along(block, axis, distance):
    devices = range(lax.axis_size(axis))
    route = [(i - distance, i) for i in devices if i - distance in devices]
    return lax.ppermute(block, axis, route)


def block_tables(width):
    counter = np.arange(width)
    signed = (counter + width // 2) % width - width // 2
    angle = 2.0 * np.pi / width * (counter[:, None] * counter[None, :] % width)
    dft = np.exp(-1j * angle) / math.sqrt(width)
    chirp = np.exp(-4j * np.pi * signed.astype(np.float64) ** 2 / (width * width))
    prop = (np.conj(dft) * chirp[None, :]) @ dft

    def right(m):
        return np.block([[m.real, m.imag], [-m.imag, m.real]])

    full = np.stack([right(dft), right(np.conj(dft)), right(prop), right(np.conj(prop))])
    full = full.astype(np.float32)
    high = full.astype(jnp.bfloat16)
    low = (full - high.astype(np.float32)).astype(jnp.bfloat16)
    return high, low


def halves(x):
    high = x.astype(jnp.bfloat16)
    low = (x - high.astype(jnp.float32)).astype(jnp.bfloat16)
    return high, low


def dot3(a, b):
    def dot(x, y):
        return jnp.dot(x, y, preferred_element_type=jnp.float32)

    return dot(a[0], b[0]) + (dot(a[0], b[1]) + dot(a[1], b[0]))


def both_sides(real, imag, high, low, which):
    width = real.shape[0]
    wide = jnp.concatenate([real, imag], axis=1)
    wide = dot3(halves(wide), (high[which], low[which]))
    tall = jnp.concatenate([wide[:, :width], wide[:, width:]], axis=0)
    other = which ^ 1
    tall = dot3((high[other], low[other]), halves(tall))
    return tall[:width], tall[width:]


def turn(window):
    y = (0.5 * SIGMA) * window
    z = y * y
    sine = -1.0 / 39916800.0
    for c in (1.0 / 362880.0, -1.0 / 5040.0, 1.0 / 120.0, -1.0 / 6.0, 1.0):
        sine = sine * z + c
    sine = sine * y
    cosine = 1.0 / 479001600.0
    for c in (-1.0 / 3628800.0, 1.0 / 40320.0, -1.0 / 720.0, 1.0 / 24.0, -0.5, 1.0):
        cosine = cosine * z + c
    return 1.0 - 2.0 * sine * sine, 2.0 * sine * cosine


def probes_kernel(corner_ref, ext_ref, illum_ref, meas_ref, high, low, acc_ref):
    width = illum_ref.shape[1]
    rows, cols = ext_ref.shape[1], ext_ref.shape[2]
    span = width + ALIGN
    acc_ref[...] = jnp.zeros_like(acc_ref)

    def probe(p, carry):
        r = corner_ref[p, 0]
        c = corner_ref[p, 1]
        base = pl.multiple_of(jnp.minimum((r // ALIGN) * ALIGN, rows - span), ALIGN)
        shift = r - base

        def cut(s):
            x = ext_ref[s, pl.ds(base, span), :].astype(jnp.float32)
            x = pltpu.roll(x, span - shift, 0)[:width]
            return pltpu.roll(x, cols - c, 1)[:, :width]

        def paste(s, g):
            x = jnp.concatenate([g, jnp.zeros((width, cols - width), jnp.float32)], axis=1)
            x = pltpu.roll(x, c, 1)
            x = jnp.concatenate([x, jnp.zeros((ALIGN, cols), jnp.float32)], axis=0)
            acc_ref[s, pl.ds(base, span), :] += pltpu.roll(x, shift, 0)

        cos0, sin0 = turn(cut(0))
        first_r = illum_ref[0] * cos0 - illum_ref[1] * sin0
        first_i = illum_ref[0] * sin0 + illum_ref[1] * cos0
        mid_r, mid_i = both_sides(first_r, first_i, high, low, 2)
        cos1, sin1 = turn(cut(1))
        exit_r = mid_r * cos1 - mid_i * sin1
        exit_i = mid_r * sin1 + mid_i * cos1
        far_r, far_i = both_sides(exit_r, exit_i, high, low, 0)
        misfit = far_r * far_r + far_i * far_i - meas_ref[p]
        scale = (4.0 * LOSS_WEIGHT) * misfit
        g_r, g_i = both_sides(scale * far_r, scale * far_i, high, low, 1)
        paste(1, SIGMA * (g_i * exit_r - g_r * exit_i))
        b_r = g_r * cos1 + g_i * sin1
        b_i = g_i * cos1 - g_r * sin1
        g_r, g_i = both_sides(b_r, b_i, high, low, 3)
        paste(0, SIGMA * (g_i * first_r - g_r * first_i))
        return carry

    lax.fori_loop(0, meas_ref.shape[0], probe, 0)


def probe_gradients(corners, extended, illumination, measured, interpret=False):
    high, low = block_tables(illumination.shape[1])
    vmem = pl.BlockSpec(memory_space=pltpu.VMEM)
    probes, width = measured.shape[0], measured.shape[1]
    flops = probes * 4 * 2 * 3 * 2 * (2 * width) ** 2 * width
    return pl.pallas_call(
        probes_kernel,
        out_shape=jax.ShapeDtypeStruct(extended.shape, jnp.float32),
        in_specs=[pl.BlockSpec(memory_space=pltpu.SMEM)] + [vmem] * 5,
        out_specs=vmem,
        compiler_params=pltpu.CompilerParams(vmem_limit_bytes=56 * 2**20),
        cost_estimate=pl.CostEstimate(flops=flops, bytes_accessed=16 * 2**20, transcendentals=0),
        interpret=interpret,
    )(corners, extended, illumination, measured, jnp.asarray(high), jnp.asarray(low))


def places():
    tile, owner = lax.axis_index("tile"), lax.axis_index("owner")
    partner = owner + 1 - 2 * (owner % 2)
    return tile, owner, partner, tile % TX != 0, tile % TX != TX - 1


def greet(owners):
    tile, owner, partner, has_left, has_right = places()
    barrier = pltpu.get_barrier_semaphore()

    def hello(device):
        pl.semaphore_signal(barrier, inc=1, device_id=device, device_id_type=MESH)

    hello({"owner": partner})
    for j in range(1, owners // 2):
        hello({"owner": (owner + 2 * j) % owners})
    pl.when(has_left)(lambda: hello({"tile": tile - 1}))
    pl.when(has_right)(lambda: hello({"tile": tile + 1}))
    beside = has_left.astype(jnp.int32) + has_right.astype(jnp.int32)
    pl.semaphore_wait(barrier, owners // 2 + beside)


def gather_kernel(owners, part_ref, ext_ref, send, recv):
    tile, owner, partner, has_left, has_right = places()
    layers, size, width = part_ref.shape
    chips = owners // 2
    peers = range(1, chips)

    def spot(s, who, side):
        start = pl.multiple_of(who * size, size)
        return ext_ref.at[s, pl.ds(start, size), pl.ds(side * width, width)]

    def copy(s, kind, src, dst, device):
        return pltpu.make_async_remote_copy(
            src_ref=src, dst_ref=dst, send_sem=send.at[s, kind], recv_sem=recv.at[s, kind],
            device_id=device, device_id_type=MESH,
        )

    def to_left(s):
        return copy(s, 0, part_ref.at[s], spot(s, owner, 1), {"tile": tile - 1})

    def to_partner(s, side):
        src = part_ref.at[s] if side == 0 else spot(s, owner, 1)
        return copy(s, 1 + side, src, spot(s, owner, side), {"owner": partner})

    def to_peer(s, side, j):
        src = part_ref.at[s] if side == 0 else spot(s, owner, 1)
        kind = 3 + side * (chips - 1) + j - 1
        return copy(s, kind, src, spot(s, owner, side), {"owner": (owner + 2 * j) % owners})

    def onward(s, side, j):
        block = spot(s, (owner + owners - 2 * j) % owners, side)
        kind = 3 + (2 + side) * (chips - 1) + j - 1
        return copy(s, kind, block, block, {"owner": partner})

    greet(owners)

    def spread(s, side):
        for j in peers:
            to_peer(s, side, j).start()
        to_partner(s, side).start()

    def pass_on(s, side):
        for j in peers:
            to_peer(s, side, j).wait_recv()
            onward(s, side, j).start()

    def finish(s, side):
        to_partner(s, side).wait()
        for j in peers:
            to_peer(s, side, j).wait_send()
            onward(s, side, j).wait()

    for s in range(layers):
        pl.when(has_left)(lambda s=s: to_left(s).start())
    spread(0, 0)
    for s in range(layers):
        @pl.when(has_right)
        def _(s=s):
            to_left(s).wait_recv()
            spread(s, 1)

        if s + 1 < layers:
            spread(s + 1, 0)
        ext_ref[s, pl.ds(pl.multiple_of(owner * size, size), size), :width] = part_ref[s]

        @pl.when(jnp.logical_not(has_right))
        def _(s=s):
            ext_ref[s, :, width:] = jnp.zeros((ext_ref.shape[1], width), ext_ref.dtype)

    for s in range(layers):
        pass_on(s, 0)
        pl.when(has_right)(lambda s=s: pass_on(s, 1))
    for s in range(layers):
        finish(s, 0)
        pl.when(has_right)(lambda s=s: finish(s, 1))
        pl.when(has_left)(lambda s=s: to_left(s).wait_send())


def gather_grid(rows_part):
    owners = lax.axis_size("owner")
    layers, size, width = rows_part.shape
    kinds = 3 + 4 * (owners // 2 - 1)
    vmem = pl.BlockSpec(memory_space=pltpu.VMEM)
    return pl.pallas_call(
        functools.partial(gather_kernel, owners),
        out_shape=jax.ShapeDtypeStruct((layers, owners * size, 2 * width), rows_part.dtype),
        in_specs=[vmem],
        out_specs=vmem,
        scratch_shapes=[pltpu.SemaphoreType.DMA((layers, kinds))] * 2,
        compiler_params=pltpu.CompilerParams(
            collective_id=0, has_side_effects=True, vmem_limit_bytes=56 * 2**20
        ),
    )(rows_part)


def reduce_kernel(owners, grad_ref, out_ref, near, total, far, edge, edge_in, sends, recvs):
    tile, owner, partner, has_left, has_right = places()
    layers, size, width = out_ref.shape
    chips = owners // 2
    order = [(s, side) for side in (1, 0) for s in range(layers)]

    def rows(who):
        return pl.ds(pl.multiple_of(who * size, size), size)

    def cols(side):
        return pl.ds(side * width, width)

    def to_partner(s, side, j):
        src = grad_ref.at[s, rows((partner + 2 * j) % owners), cols(side)]
        return pltpu.make_async_remote_copy(
            src_ref=src, dst_ref=near.at[s, side, j],
            send_sem=sends.at[s, side, j], recv_sem=recvs.at[s, side, j],
            device_id={"owner": partner}, device_id_type=MESH,
        )

    def to_peer(s, side, j):
        return pltpu.make_async_remote_copy(
            src_ref=total.at[s, side, j - 1], dst_ref=far.at[s, side, j - 1],
            send_sem=sends.at[s, side, chips + j - 1], recv_sem=recvs.at[s, side, chips + j - 1],
            device_id={"owner": (owner + 2 * j) % owners}, device_id_type=MESH,
        )

    def to_right(s):
        return pltpu.make_async_remote_copy(
            src_ref=edge.at[s], dst_ref=edge_in.at[s],
            send_sem=sends.at[s, 0, 2 * chips - 1], recv_sem=recvs.at[s, 0, 2 * chips - 1],
            device_id={"tile": tile + 1}, device_id_type=MESH,
        )

    greet(owners)
    peers = list(range(1, chips))
    for s, side in order:
        for j in peers + [0]:
            to_partner(s, side, j).start()
    for s, side in order:
        for j in peers:
            to_partner(s, side, j).wait_recv()
            own = grad_ref[s, rows((owner + 2 * j) % owners), cols(side)]
            total[s, side, j - 1] = own + near[s, side, j]
            to_peer(s, side, j).start()
    for s, side in order:
        to_partner(s, side, 0).wait_recv()
        value = grad_ref[s, rows(owner), cols(side)] + near[s, side, 0]
        for j in peers:
            to_peer(s, side, j).wait_recv()
            value = value + far[s, side, j - 1]
        if side == 1:
            edge[s] = value
            pl.when(has_right)(lambda s=s: to_right(s).start())
        else:
            out_ref[s] = value
    for s in range(layers):
        @pl.when(has_left)
        def _(s=s):
            to_right(s).wait_recv()
            out_ref[s] += edge_in[s]

    for s, side in order:
        for j in peers + [0]:
            to_partner(s, side, j).wait_send()
        for j in peers:
            to_peer(s, side, j).wait_send()
    for s in range(layers):
        pl.when(has_right)(lambda s=s: to_right(s).wait_send())


def reduce_grid(wide_grad):
    owners = lax.axis_size("owner")
    layers, tile_rows, cols = wide_grad.shape
    size, width, chips = tile_rows // owners, cols // 2, owners // 2
    vmem = pl.BlockSpec(memory_space=pltpu.VMEM)
    block = (size, width)
    return pl.pallas_call(
        functools.partial(reduce_kernel, owners),
        out_shape=jax.ShapeDtypeStruct((layers,) + block, jnp.float32),
        in_specs=[vmem],
        out_specs=vmem,
        scratch_shapes=[
            pltpu.VMEM((layers, 2, chips) + block, jnp.float32),
            pltpu.VMEM((layers, 2, max(chips - 1, 1)) + block, jnp.float32),
            pltpu.VMEM((layers, 2, max(chips - 1, 1)) + block, jnp.float32),
            pltpu.VMEM((layers,) + block, jnp.float32),
            pltpu.VMEM((layers,) + block, jnp.float32),
            pltpu.SemaphoreType.DMA((layers, 2, 2 * chips)),
            pltpu.SemaphoreType.DMA((layers, 2, 2 * chips)),
        ],
        compiler_params=pltpu.CompilerParams(
            collective_id=1, has_side_effects=True, vmem_limit_bytes=56 * 2**20
        ),
    )(wide_grad)


def body(potential, positions, illumination, measured):
    probe_width = illumination.shape[1]
    rows_part = potential[:, 0]
    tile_rows = rows_part.shape[1] * lax.axis_size("owner")
    tile_cols = rows_part.shape[2]
    below = lax.axis_size("tile") > TX
    extended = gather_grid(rows_part)
    if below:
        lower_rim = passed_along(extended[:, :probe_width, :], "tile", -TX)
        extended = jnp.concatenate([extended, lower_rim], axis=1)
    tile_id = lax.axis_index("tile")
    first = jnp.stack([tile_id // TX * tile_rows, tile_id % TX * tile_cols])
    corners = positions - first[None, :].astype(jnp.int32)
    accumulated = probe_gradients(corners, extended, illumination, measured)
    wide_grad = accumulated[:, :tile_rows, :]
    if below:
        upper_back = passed_along(accumulated[:, tile_rows:, :], "tile", TX)
        wide_grad = wide_grad.at[:, :probe_width, :].add(upper_back)
    return reduce_grid(wide_grad)[:, None]


def solution(mesh):
    in_specs = (
        P(None, "tile", "owner", None),
        P(("tile", "owner"), None),
        P(),
        P(("tile", "owner"), None, None),
    )
    out_specs = P(None, "tile", "owner", None)
    return jax.shard_map(body, mesh=mesh, in_specs=in_specs, out_specs=out_specs, check_vma=False)
```

```python
import functools
import math

import jax
import jax.numpy as jnp
import numpy as np
from jax import lax
from jax.experimental import pallas as pl
from jax.experimental.pallas import tpu as pltpu
from jax.sharding import PartitionSpec as P

TX = 8

SIGMA = 0.5
LOSS_WEIGHT = 0.125
ALIGN = 16
MESH = pl.DeviceIdType.MESH


def passed_along(block, axis, distance):
    devices = range(lax.axis_size(axis))
    route = [(i - distance, i) for i in devices if i - distance in devices]
    return lax.ppermute(block, axis, route)


def block_tables(width):
    counter = np.arange(width)
    signed = (counter + width // 2) % width - width // 2
    angle = 2.0 * np.pi / width * (counter[:, None] * counter[None, :] % width)
    dft = np.exp(-1j * angle) / math.sqrt(width)
    chirp = np.exp(-4j * np.pi * signed.astype(np.float64) ** 2 / (width * width))
    prop = (np.conj(dft) * chirp[None, :]) @ dft

    def right(m):
        return np.block([[m.real, m.imag], [-m.imag, m.real]])

    full = np.stack([right(dft), right(np.conj(dft)), right(prop), right(np.conj(prop))])
    full = full.astype(np.float32)
    high = full.astype(jnp.bfloat16)
    low = (full - high.astype(np.float32)).astype(jnp.bfloat16)
    return high, low


def halves(x):
    high = x.astype(jnp.bfloat16)
    low = (x - high.astype(jnp.float32)).astype(jnp.bfloat16)
    return high, low


def dot3(a, b):
    def dot(x, y):
        return jnp.dot(x, y, preferred_element_type=jnp.float32)

    return dot(a[0], b[0]) + (dot(a[0], b[1]) + dot(a[1], b[0]))


def both_sides(real, imag, high, low, which):
    width = real.shape[0]
    wide = jnp.concatenate([real, imag], axis=1)
    wide = dot3(halves(wide), (high[which], low[which]))
    tall = jnp.concatenate([wide[:, :width], wide[:, width:]], axis=0)
    other = which ^ 1
    tall = dot3((high[other], low[other]), halves(tall))
    return tall[:width], tall[width:]


def turn(window):
    y = (0.5 * SIGMA) * window
    z = y * y
    sine = -1.0 / 39916800.0
    for c in (1.0 / 362880.0, -1.0 / 5040.0, 1.0 / 120.0, -1.0 / 6.0, 1.0):
        sine = sine * z + c
    sine = sine * y
    cosine = 1.0 / 479001600.0
    for c in (-1.0 / 3628800.0, 1.0 / 40320.0, -1.0 / 720.0, 1.0 / 24.0, -0.5, 1.0):
        cosine = cosine * z + c
    return 1.0 - 2.0 * sine * sine, 2.0 * sine * cosine


def probes_kernel(corner_ref, ext_ref, illum_ref, meas_ref, high, low, acc_ref):
    width = illum_ref.shape[1]
    rows, cols = ext_ref.shape[1], ext_ref.shape[2]
    span = width + ALIGN
    acc_ref[...] = jnp.zeros_like(acc_ref)

    def probe(p, carry):
        r = corner_ref[p, 0]
        c = corner_ref[p, 1]
        base = pl.multiple_of(jnp.minimum((r // ALIGN) * ALIGN, rows - span), ALIGN)
        shift = r - base

        def cut(s):
            x = ext_ref[s, pl.ds(base, span), :].astype(jnp.float32)
            x = pltpu.roll(x, span - shift, 0)[:width]
            return pltpu.roll(x, cols - c, 1)[:, :width]

        def paste(s, g):
            x = jnp.concatenate([g, jnp.zeros((width, cols - width), jnp.float32)], axis=1)
            x = pltpu.roll(x, c, 1)
            x = jnp.concatenate([x, jnp.zeros((ALIGN, cols), jnp.float32)], axis=0)
            acc_ref[s, pl.ds(base, span), :] += pltpu.roll(x, shift, 0)

        cos0, sin0 = turn(cut(0))
        first_r = illum_ref[0] * cos0 - illum_ref[1] * sin0
        first_i = illum_ref[0] * sin0 + illum_ref[1] * cos0
        mid_r, mid_i = both_sides(first_r, first_i, high, low, 2)
        cos1, sin1 = turn(cut(1))
        exit_r = mid_r * cos1 - mid_i * sin1
        exit_i = mid_r * sin1 + mid_i * cos1
        far_r, far_i = both_sides(exit_r, exit_i, high, low, 0)
        misfit = far_r * far_r + far_i * far_i - meas_ref[p]
        scale = (4.0 * LOSS_WEIGHT) * misfit
        g_r, g_i = both_sides(scale * far_r, scale * far_i, high, low, 1)
        paste(1, SIGMA * (g_i * exit_r - g_r * exit_i))
        b_r = g_r * cos1 + g_i * sin1
        b_i = g_i * cos1 - g_r * sin1
        g_r, g_i = both_sides(b_r, b_i, high, low, 3)
        paste(0, SIGMA * (g_i * first_r - g_r * first_i))
        return carry

    lax.fori_loop(0, meas_ref.shape[0], probe, 0)


def probe_gradients(corners, extended, illumination, measured, interpret=False):
    high, low = block_tables(illumination.shape[1])
    vmem = pl.BlockSpec(memory_space=pltpu.VMEM)
    probes, width = measured.shape[0], measured.shape[1]
    flops = probes * 4 * 2 * 3 * 2 * (2 * width) ** 2 * width
    return pl.pallas_call(
        probes_kernel,
        out_shape=jax.ShapeDtypeStruct(extended.shape, jnp.float32),
        in_specs=[pl.BlockSpec(memory_space=pltpu.SMEM)] + [vmem] * 5,
        out_specs=vmem,
        compiler_params=pltpu.CompilerParams(vmem_limit_bytes=56 * 2**20),
        cost_estimate=pl.CostEstimate(flops=flops, bytes_accessed=16 * 2**20, transcendentals=0),
        interpret=interpret,
    )(corners, extended, illumination, measured, jnp.asarray(high), jnp.asarray(low))


def places():
    tile, owner = lax.axis_index("tile"), lax.axis_index("owner")
    partner = owner + 1 - 2 * (owner % 2)
    return tile, owner, partner, tile % TX != 0, tile % TX != TX - 1


def greet(owners):
    tile, owner, partner, has_left, has_right = places()
    barrier = pltpu.get_barrier_semaphore()

    def hello(device):
        pl.semaphore_signal(barrier, inc=1, device_id=device, device_id_type=MESH)

    hello({"owner": partner})
    for j in range(1, owners // 2):
        hello({"owner": (owner + 2 * j) % owners})
    pl.when(has_left)(lambda: hello({"tile": tile - 1}))
    pl.when(has_right)(lambda: hello({"tile": tile + 1}))
    beside = has_left.astype(jnp.int32) + has_right.astype(jnp.int32)
    pl.semaphore_wait(barrier, owners // 2 + beside)


def gather_kernel(owners, part_ref, ext_ref, send, recv):
    tile, owner, partner, has_left, has_right = places()
    layers, size, width = part_ref.shape
    chips = owners // 2
    peers = range(1, chips)

    def spot(s, who, side):
        start = pl.multiple_of(who * size, size)
        return ext_ref.at[s, pl.ds(start, size), pl.ds(side * width, width)]

    def copy(s, kind, src, dst, device):
        return pltpu.make_async_remote_copy(
            src_ref=src, dst_ref=dst, send_sem=send.at[s, kind], recv_sem=recv.at[s, kind],
            device_id=device, device_id_type=MESH,
        )

    def to_left(s):
        return copy(s, 0, part_ref.at[s], spot(s, owner, 1), {"tile": tile - 1})

    def to_partner(s, side):
        src = part_ref.at[s] if side == 0 else spot(s, owner, 1)
        return copy(s, 1 + side, src, spot(s, owner, side), {"owner": partner})

    def to_peer(s, side, j):
        src = part_ref.at[s] if side == 0 else spot(s, owner, 1)
        kind = 3 + side * (chips - 1) + j - 1
        return copy(s, kind, src, spot(s, owner, side), {"owner": (owner + 2 * j) % owners})

    def onward(s, side, j):
        block = spot(s, (owner + owners - 2 * j) % owners, side)
        kind = 3 + (2 + side) * (chips - 1) + j - 1
        return copy(s, kind, block, block, {"owner": partner})

    greet(owners)

    def spread(s, side):
        for j in peers:
            to_peer(s, side, j).start()
        to_partner(s, side).start()

    def pass_on(s, side):
        for j in peers:
            to_peer(s, side, j).wait_recv()
            onward(s, side, j).start()

    def finish(s, side):
        to_partner(s, side).wait()
        for j in peers:
            to_peer(s, side, j).wait_send()
            onward(s, side, j).wait()

    for s in range(layers):
        pl.when(has_left)(lambda s=s: to_left(s).start())
    spread(0, 0)
    for s in range(layers):
        @pl.when(has_right)
        def _(s=s):
            to_left(s).wait_recv()
            spread(s, 1)

        if s + 1 < layers:
            spread(s + 1, 0)
        ext_ref[s, pl.ds(pl.multiple_of(owner * size, size), size), :width] = part_ref[s]

        @pl.when(jnp.logical_not(has_right))
        def _(s=s):
            ext_ref[s, :, width:] = jnp.zeros((ext_ref.shape[1], width), ext_ref.dtype)

    for s in range(layers):
        pass_on(s, 0)
        pl.when(has_right)(lambda s=s: pass_on(s, 1))
    for s in range(layers):
        finish(s, 0)
        pl.when(has_right)(lambda s=s: finish(s, 1))
        pl.when(has_left)(lambda s=s: to_left(s).wait_send())


def gather_grid(rows_part):
    owners = lax.axis_size("owner")
    layers, size, width = rows_part.shape
    kinds = 3 + 4 * (owners // 2 - 1)
    vmem = pl.BlockSpec(memory_space=pltpu.VMEM)
    return pl.pallas_call(
        functools.partial(gather_kernel, owners),
        out_shape=jax.ShapeDtypeStruct((layers, owners * size, 2 * width), rows_part.dtype),
        in_specs=[vmem],
        out_specs=vmem,
        scratch_shapes=[pltpu.SemaphoreType.DMA((layers, kinds))] * 2,
        compiler_params=pltpu.CompilerParams(
            collective_id=0, has_side_effects=True, vmem_limit_bytes=56 * 2**20
        ),
    )(rows_part)


def reduce_kernel(owners, grad_ref, out_ref, near, total, far, edge, edge_in, sends, recvs):
    tile, owner, partner, has_left, has_right = places()
    layers, size, width = out_ref.shape
    chips = owners // 2
    order = [(s, side) for side in (1, 0) for s in range(layers)]

    def rows(who):
        return pl.ds(pl.multiple_of(who * size, size), size)

    def cols(side):
        return pl.ds(side * width, width)

    def to_partner(s, side, j):
        src = grad_ref.at[s, rows((partner + 2 * j) % owners), cols(side)]
        return pltpu.make_async_remote_copy(
            src_ref=src, dst_ref=near.at[s, side, j],
            send_sem=sends.at[s, side, j], recv_sem=recvs.at[s, side, j],
            device_id={"owner": partner}, device_id_type=MESH,
        )

    def to_peer(s, side, j):
        return pltpu.make_async_remote_copy(
            src_ref=total.at[s, side, j - 1], dst_ref=far.at[s, side, j - 1],
            send_sem=sends.at[s, side, chips + j - 1], recv_sem=recvs.at[s, side, chips + j - 1],
            device_id={"owner": (owner + 2 * j) % owners}, device_id_type=MESH,
        )

    def to_right(s):
        return pltpu.make_async_remote_copy(
            src_ref=edge.at[s], dst_ref=edge_in.at[s],
            send_sem=sends.at[s, 0, 2 * chips - 1], recv_sem=recvs.at[s, 0, 2 * chips - 1],
            device_id={"tile": tile + 1}, device_id_type=MESH,
        )

    greet(owners)
    peers = list(range(1, chips))
    for s, side in order:
        for j in peers + [0]:
            to_partner(s, side, j).start()
    for s, side in order:
        for j in peers:
            to_partner(s, side, j).wait_recv()
            own = grad_ref[s, rows((owner + 2 * j) % owners), cols(side)]
            total[s, side, j - 1] = own + near[s, side, j]
            to_peer(s, side, j).start()
    for s, side in order:
        to_partner(s, side, 0).wait_recv()
        value = grad_ref[s, rows(owner), cols(side)] + near[s, side, 0]
        for j in peers:
            to_peer(s, side, j).wait_recv()
            value = value + far[s, side, j - 1]
        if side == 1:
            edge[s] = value
            pl.when(has_right)(lambda s=s: to_right(s).start())
        else:
            out_ref[s] = value
    for s in range(layers):
        @pl.when(has_left)
        def _(s=s):
            to_right(s).wait_recv()
            out_ref[s] += edge_in[s]

    for s, side in order:
        for j in peers + [0]:
            to_partner(s, side, j).wait_send()
        for j in peers:
            to_peer(s, side, j).wait_send()
    for s in range(layers):
        pl.when(has_right)(lambda s=s: to_right(s).wait_send())


def reduce_grid(wide_grad):
    owners = lax.axis_size("owner")
    layers, tile_rows, cols = wide_grad.shape
    size, width, chips = tile_rows // owners, cols // 2, owners // 2
    vmem = pl.BlockSpec(memory_space=pltpu.VMEM)
    block = (size, width)
    return pl.pallas_call(
        functools.partial(reduce_kernel, owners),
        out_shape=jax.ShapeDtypeStruct((layers,) + block, jnp.float32),
        in_specs=[vmem],
        out_specs=vmem,
        scratch_shapes=[
            pltpu.VMEM((layers, 2, chips) + block, jnp.float32),
            pltpu.VMEM((layers, 2, max(chips - 1, 1)) + block, jnp.float32),
            pltpu.VMEM((layers, 2, max(chips - 1, 1)) + block, jnp.float32),
            pltpu.VMEM((layers,) + block, jnp.float32),
            pltpu.VMEM((layers,) + block, jnp.float32),
            pltpu.SemaphoreType.DMA((layers, 2, 2 * chips)),
            pltpu.SemaphoreType.DMA((layers, 2, 2 * chips)),
        ],
        compiler_params=pltpu.CompilerParams(
            collective_id=1, has_side_effects=True, vmem_limit_bytes=56 * 2**20
        ),
    )(wide_grad)


def fused_kernel(
    owners, place_ref, part_ref, illum_ref, meas_hbm, high_hbm, low_hbm, out_ref,
    ext0, ext1, meas_ref, high, low, first, back, pads, grad, near, total, far, edge, edge_in,
    loads, g_send, g_recv, sends, recvs,
):
    tile, owner, partner, has_left, has_right = places()
    layers, groups, _, width = part_ref.shape
    size = groups * ALIGN
    chips = owners // 2
    peers = list(range(1, chips))
    probes = meas_ref.shape[0]
    cols_all = 2 * width
    rows_all = owners * size
    span = width + ALIGN
    ext = (ext0, ext1)
    tail = width + 8

    fetches = [
        pltpu.make_async_copy(src, dst, loads.at[i])
        for i, (src, dst) in enumerate(((high_hbm, high), (low_hbm, low), (meas_hbm, meas_ref)))
    ]
    for fetch in fetches:
        fetch.start()
    greet(owners)

    def spot(s, who, side):
        return ext[s].at[pl.ds(who * groups, groups), :, pl.ds(side * width, width)]

    def g_copy(s, kind, src, dst, device):
        return pltpu.make_async_remote_copy(
            src_ref=src, dst_ref=dst, send_sem=g_send.at[s, kind], recv_sem=g_recv.at[s, kind],
            device_id=device, device_id_type=MESH,
        )

    def own(s, side):
        return part_ref.at[s] if side == 0 else spot(s, owner, 1)

    def g_left(s):
        return g_copy(s, 0, part_ref.at[s], spot(s, owner, 1), {"tile": tile - 1})

    def g_partner(s, side):
        return g_copy(s, 1 + side, own(s, side), spot(s, owner, side), {"owner": partner})

    def g_peer(s, side, j):
        kind = 3 + side * (chips - 1) + j - 1
        device = {"owner": (owner + 2 * j) % owners}
        return g_copy(s, kind, own(s, side), spot(s, owner, side), device)

    def g_onward(s, side, j):
        block = spot(s, (owner + owners - 2 * j) % owners, side)
        kind = 3 + (2 + side) * (chips - 1) + j - 1
        return g_copy(s, kind, block, block, {"owner": partner})

    def spread(s, side):
        for j in peers:
            g_peer(s, side, j).start()
        g_partner(s, side).start()

    def pass_on(s, side):
        for j in peers:
            g_peer(s, side, j).wait_recv()
            g_onward(s, side, j).start()

    def landed(s, side):
        g_partner(s, side).wait_recv()
        for j in peers:
            g_onward(s, side, j).wait_recv()

    def sent(s, side):
        g_partner(s, side).wait_send()
        for j in peers:
            g_peer(s, side, j).wait_send()
            g_onward(s, side, j).wait_send()

    def right_spread(s):
        g_left(s).wait_recv()
        spread(s, 1)

    for s in range(layers):
        pl.when(has_left)(lambda s=s: g_left(s).start())
    spread(0, 0)
    blank = jnp.zeros((probes, size // 8, 8, cols_all), jnp.float32)
    pads[:, : size // 8] = blank
    pads[:, (size + tail) // 8 :] = blank
    for s in range(layers):
        ext[s][pl.ds(owner * groups, groups), :, :width] = part_ref[s]

        @pl.when(jnp.logical_not(has_right))
        def _(s=s):
            ext[s][:, :, width:] = jnp.zeros((rows_all // ALIGN, ALIGN, width), part_ref.dtype)

    pl.when(has_right)(lambda: right_spread(0))
    spread(1, 0)
    pass_on(0, 0)
    pl.when(has_right)(lambda: pass_on(0, 1))
    pl.when(has_right)(lambda: right_spread(1))
    pass_on(1, 0)
    pl.when(has_right)(lambda: pass_on(1, 1))
    for s in range(layers):
        landed(s, 0)
        pl.when(has_right)(lambda s=s: landed(s, 1))
    for fetch in fetches:
        fetch.wait()

    def pick(shape, dim, shift):
        along = lax.broadcasted_iota(jnp.int32, shape, dim)
        other = lax.broadcasted_iota(jnp.int32, shape, 1 - dim)
        return jnp.where(along == other + shift, 1.0, 0.0).astype(jnp.bfloat16)

    def dot(x, y):
        return jnp.dot(x, y, preferred_element_type=jnp.float32)

    def cut(s, p):
        base = place_ref[p, 0]
        x = jnp.concatenate([ext[s][base + i] for i in range(span // ALIGN)], axis=0)
        x = dot(x, pick((cols_all, width), 0, place_ref[p, 2])).astype(jnp.bfloat16)
        return dot(pick((width, span), 1, place_ref[p, 1]), x)

    def paste(p, g):
        down = pick((tail, width), 0, place_ref[p, 3])
        a, b = halves(g)
        a, b = halves(dot(down, a) + dot(down, b))
        along = pick((width, cols_all), 1, place_ref[p, 2])
        value = dot(a, along) + dot(b, along)
        pads[p, pl.ds(size // 8, tail // 8)] = value.reshape(tail // 8, 8, cols_all)

    def forward(p, carry):
        cos0, sin0 = turn(cut(0, p))
        first_r = illum_ref[0] * cos0 - illum_ref[1] * sin0
        first_i = illum_ref[0] * sin0 + illum_ref[1] * cos0
        first[p, 0] = first_r
        first[p, 1] = first_i
        mid_r, mid_i = both_sides(first_r, first_i, high, low, 2)
        cos1, sin1 = turn(cut(1, p))
        exit_r = mid_r * cos1 - mid_i * sin1
        exit_i = mid_r * sin1 + mid_i * cos1
        far_r, far_i = both_sides(exit_r, exit_i, high, low, 0)
        misfit = far_r * far_r + far_i * far_i - meas_ref[p]
        scale = (4.0 * LOSS_WEIGHT) * misfit
        g_r, g_i = both_sides(scale * far_r, scale * far_i, high, low, 1)
        paste(p, SIGMA * (g_i * exit_r - g_r * exit_i))
        back[p, 0] = g_r * cos1 + g_i * sin1
        back[p, 1] = g_i * cos1 - g_r * sin1
        return carry

    def backward(p, carry):
        g_r, g_i = both_sides(back[p, 0], back[p, 1], high, low, 3)
        paste(p, SIGMA * (g_i * first[p, 0] - g_r * first[p, 1]))
        return carry

    def rows(who):
        return pl.ds(pl.multiple_of(who * size, size), size)

    def cols(side):
        return pl.ds(side * width, width)

    def r_copy(s, kind, src, dst, device):
        return pltpu.make_async_remote_copy(
            src_ref=src, dst_ref=dst, send_sem=sends.at[s, kind], recv_sem=recvs.at[s, kind],
            device_id=device, device_id_type=MESH,
        )

    def to_partner(s, side, j):
        src = grad.at[s, rows((partner + 2 * j) % owners), cols(side)]
        return r_copy(s, side * chips + j, src, near.at[s, side, j], {"owner": partner})

    def to_peer(s, side, j):
        kind = 2 * chips + side * (chips - 1) + j - 1
        device = {"owner": (owner + 2 * j) % owners}
        return r_copy(s, kind, total.at[s, side, j - 1], far.at[s, side, j - 1], device)

    def to_right(s):
        return r_copy(s, 4 * chips - 2, edge.at[s], edge_in.at[s], {"tile": tile + 1})

    def block_sum(who, side):
        starts = [place_ref[p, 4 + who] for p in range(probes)]
        parts = []
        for i in range(size // 8):
            terms = [pads[p, starts[p] + i, :, cols(side)] for p in range(probes)]
            parts.append(functools.reduce(jnp.add, terms))
        value = jnp.concatenate(parts, axis=0)
        return value

    def give(s):
        for side in (1, 0):
            for j in peers + [0]:
                who = (partner + 2 * j) % owners
                grad[s, rows(who), cols(side)] = block_sum(who, side)
                to_partner(s, side, j).start()
        for side in (1, 0):
            for j in peers + [0]:
                who = (owner + 2 * j) % owners
                grad[s, rows(who), cols(side)] = block_sum(who, side)

    def across(s):
        for side in (1, 0):
            for j in peers:
                to_partner(s, side, j).wait_recv()
                mine = grad[s, rows((owner + 2 * j) % owners), cols(side)]
                total[s, side, j - 1] = mine + near[s, side, j]
                to_peer(s, side, j).start()

    def collect(s, side):
        to_partner(s, side, 0).wait_recv()
        value = grad[s, rows(owner), cols(side)] + near[s, side, 0]
        for j in peers:
            to_peer(s, side, j).wait_recv()
            value = value + far[s, side, j - 1]
        if side == 1:
            edge[s] = value
            pl.when(has_right)(lambda: to_right(s).start())
        else:
            out_ref[s] = value

    def add_edge(s):
        to_right(s).wait_recv()
        out_ref[s] += edge_in[s]

    lax.fori_loop(0, probes, forward, 0)
    give(1)
    lax.fori_loop(0, 1, backward, 0)
    across(1)
    lax.fori_loop(1, probes, backward, 0)
    give(0)
    across(0)
    for side in (1, 0):
        for s in (1, 0):
            collect(s, side)
    for s in (1, 0):
        pl.when(has_left)(lambda s=s: add_edge(s))

    for s in range(layers):
        sent(s, 0)
        pl.when(has_right)(lambda s=s: sent(s, 1))
        pl.when(has_left)(lambda s=s: g_left(s).wait_send())
        for side in (0, 1):
            for j in peers + [0]:
                to_partner(s, side, j).wait_send()
            for j in peers:
                to_peer(s, side, j).wait_send()
        pl.when(has_right)(lambda s=s: to_right(s).wait_send())


def fused(rows_part, positions, illumination, measured):
    owners = lax.axis_size("owner")
    layers, size, width = rows_part.shape
    probes = measured.shape[0]
    chips = owners // 2
    peers = max(chips - 1, 1)
    high, low = block_tables(width)
    tile = lax.axis_index("tile")
    row = positions[:, 0] - tile // TX * (owners * size)
    col = positions[:, 1] - tile % TX * width
    base = jnp.minimum(row // ALIGN * ALIGN, owners * size - width - ALIGN)
    starts = size + jnp.arange(owners)[None, :] * size - (row // 8 * 8)[:, None]
    starts = jnp.clip(starts, 0, size + width + 8)
    heads = jnp.stack([base // ALIGN, row - base, col, row % 8], axis=1)
    place = jnp.concatenate([heads, starts // 8], axis=1)
    place = place.astype(jnp.int32)
    grouped = rows_part.reshape(layers, size // ALIGN, ALIGN, width)
    vmem = pl.BlockSpec(memory_space=pltpu.VMEM)
    anywhere = pl.BlockSpec(memory_space=pl.ANY)
    block = (size, width)
    f32 = jnp.float32
    flops = probes * 4 * 2 * 3 * 2 * (2 * width) ** 2 * width
    return pl.pallas_call(
        functools.partial(fused_kernel, owners),
        out_shape=jax.ShapeDtypeStruct((layers,) + block, f32),
        in_specs=[pl.BlockSpec(memory_space=pltpu.SMEM), vmem, vmem] + [anywhere] * 3,
        out_specs=vmem,
        scratch_shapes=[
            pltpu.VMEM((owners * size // ALIGN, ALIGN, 2 * width), rows_part.dtype),
            pltpu.VMEM((owners * size // ALIGN, ALIGN, 2 * width), rows_part.dtype),
            pltpu.VMEM(measured.shape, f32),
            pltpu.VMEM(high.shape, jnp.bfloat16),
            pltpu.VMEM(low.shape, jnp.bfloat16),
            pltpu.VMEM((probes, 2, width, width), f32),
            pltpu.VMEM((probes, 2, width, width), f32),
            pltpu.VMEM((probes, (2 * size + width) // 8 + 1, 8, 2 * width), f32),
            pltpu.VMEM((layers, owners * size, 2 * width), f32),
            pltpu.VMEM((layers, 2, chips) + block, f32),
            pltpu.VMEM((layers, 2, peers) + block, f32),
            pltpu.VMEM((layers, 2, peers) + block, f32),
            pltpu.VMEM((layers,) + block, f32),
            pltpu.VMEM((layers,) + block, f32),
            pltpu.SemaphoreType.DMA((3,)),
            pltpu.SemaphoreType.DMA((layers, 3 + 4 * (chips - 1))),
            pltpu.SemaphoreType.DMA((layers, 3 + 4 * (chips - 1))),
            pltpu.SemaphoreType.DMA((layers, 4 * chips - 1)),
            pltpu.SemaphoreType.DMA((layers, 4 * chips - 1)),
        ],
        compiler_params=pltpu.CompilerParams(
            collective_id=2, has_side_effects=True, vmem_limit_bytes=56 * 2**20
        ),
        cost_estimate=pl.CostEstimate(flops=flops, bytes_accessed=8 * 2**20, transcendentals=0),
    )(place, grouped, illumination, measured, jnp.asarray(high), jnp.asarray(low))


def body(potential, positions, illumination, measured):
    probe_width = illumination.shape[1]
    rows_part = potential[:, 0]
    layers = rows_part.shape[0]
    tile_rows = rows_part.shape[1] * lax.axis_size("owner")
    tile_cols = rows_part.shape[2]
    below = lax.axis_size("tile") > TX
    if not below and layers == 2:
        return fused(rows_part, positions, illumination, measured)[:, None]
    extended = gather_grid(rows_part)
    if below:
        lower_rim = passed_along(extended[:, :probe_width, :], "tile", -TX)
        extended = jnp.concatenate([extended, lower_rim], axis=1)
    tile_id = lax.axis_index("tile")
    first = jnp.stack([tile_id // TX * tile_rows, tile_id % TX * tile_cols])
    corners = positions - first[None, :].astype(jnp.int32)
    accumulated = probe_gradients(corners, extended, illumination, measured)
    wide_grad = accumulated[:, :tile_rows, :]
    if below:
        upper_back = passed_along(accumulated[:, tile_rows:, :], "tile", TX)
        wide_grad = wide_grad.at[:, :probe_width, :].add(upper_back)
    return reduce_grid(wide_grad)[:, None]


def solution(mesh):
    in_specs = (
        P(None, "tile", "owner", None),
        P(("tile", "owner"), None),
        P(),
        P(("tile", "owner"), None, None),
    )
    out_specs = P(None, "tile", "owner", None)
    return jax.shard_map(body, mesh=mesh, in_specs=in_specs, out_specs=out_specs, check_vma=False)
```

```python
import functools
import math

import jax
import jax.numpy as jnp
import numpy as np
from jax import lax
from jax.experimental import pallas as pl
from jax.experimental.pallas import tpu as pltpu
from jax.sharding import PartitionSpec as P

TX = 8

SIGMA = 0.5
LOSS_WEIGHT = 0.125
ALIGN = 16
GROUP = 2
MESH = pl.DeviceIdType.MESH


def passed_along(block, axis, distance):
    devices = range(lax.axis_size(axis))
    route = [(i - distance, i) for i in devices if i - distance in devices]
    return lax.ppermute(block, axis, route)


def block_tables(width):
    counter = np.arange(width)
    signed = (counter + width // 2) % width - width // 2
    angle = 2.0 * np.pi / width * (counter[:, None] * counter[None, :] % width)
    dft = np.exp(-1j * angle) / math.sqrt(width)
    chirp = np.exp(-4j * np.pi * signed.astype(np.float64) ** 2 / (width * width))
    prop = (np.conj(dft) * chirp[None, :]) @ dft

    def right(m):
        return np.block([[m.real, m.imag], [-m.imag, m.real]])

    full = np.stack([right(dft), right(np.conj(dft)), right(prop), right(np.conj(prop))])
    full = full.astype(np.float32)
    high = full.astype(jnp.bfloat16)
    low = (full - high.astype(np.float32)).astype(jnp.bfloat16)
    return high, low


def halves(x):
    high = x.astype(jnp.bfloat16)
    low = (x - high.astype(jnp.float32)).astype(jnp.bfloat16)
    return high, low


def dot3(a, b):
    def dot(x, y):
        return jnp.dot(x, y, preferred_element_type=jnp.float32)

    return dot(a[0], b[0]) + (dot(a[0], b[1]) + dot(a[1], b[0]))


def both_sides(real, imag, high, low, which):
    width = real.shape[0]
    wide = jnp.concatenate([real, imag], axis=1)
    wide = dot3(halves(wide), (high[which], low[which]))
    tall = jnp.concatenate([wide[:, :width], wide[:, width:]], axis=0)
    other = which ^ 1
    tall = dot3((high[other], low[other]), halves(tall))
    return tall[:width], tall[width:]


def both_sides_of(waves, high, low, which):
    width = waves[0][0].shape[0]
    wide = jnp.concatenate([jnp.concatenate(wave, axis=1) for wave in waves], axis=0)
    wide = dot3(halves(wide), (high[which], low[which]))
    spans = [slice(k * width, (k + 1) * width) for k in range(len(waves))]
    real = jnp.concatenate([wide[span, :width] for span in spans], axis=1)
    imag = jnp.concatenate([wide[span, width:] for span in spans], axis=1)
    tall = jnp.concatenate([real, imag], axis=0)
    other = which ^ 1
    tall = dot3((high[other], low[other]), halves(tall))
    return [(tall[:width, span], tall[width:, span]) for span in spans]


def turn(window):
    y = (0.5 * SIGMA) * window
    z = y * y
    sine = -1.0 / 39916800.0
    for c in (1.0 / 362880.0, -1.0 / 5040.0, 1.0 / 120.0, -1.0 / 6.0, 1.0):
        sine = sine * z + c
    sine = sine * y
    cosine = 1.0 / 479001600.0
    for c in (-1.0 / 3628800.0, 1.0 / 40320.0, -1.0 / 720.0, 1.0 / 24.0, -0.5, 1.0):
        cosine = cosine * z + c
    return 1.0 - 2.0 * sine * sine, 2.0 * sine * cosine


def probes_kernel(corner_ref, ext_ref, illum_ref, meas_ref, high, low, acc_ref):
    width = illum_ref.shape[1]
    rows, cols = ext_ref.shape[1], ext_ref.shape[2]
    span = width + ALIGN
    acc_ref[...] = jnp.zeros_like(acc_ref)

    def probe(p, carry):
        r = corner_ref[p, 0]
        c = corner_ref[p, 1]
        base = pl.multiple_of(jnp.minimum((r // ALIGN) * ALIGN, rows - span), ALIGN)
        shift = r - base

        def cut(s):
            x = ext_ref[s, pl.ds(base, span), :].astype(jnp.float32)
            x = pltpu.roll(x, span - shift, 0)[:width]
            return pltpu.roll(x, cols - c, 1)[:, :width]

        def paste(s, g):
            x = jnp.concatenate([g, jnp.zeros((width, cols - width), jnp.float32)], axis=1)
            x = pltpu.roll(x, c, 1)
            x = jnp.concatenate([x, jnp.zeros((ALIGN, cols), jnp.float32)], axis=0)
            acc_ref[s, pl.ds(base, span), :] += pltpu.roll(x, shift, 0)

        cos0, sin0 = turn(cut(0))
        first_r = illum_ref[0] * cos0 - illum_ref[1] * sin0
        first_i = illum_ref[0] * sin0 + illum_ref[1] * cos0
        mid_r, mid_i = both_sides(first_r, first_i, high, low, 2)
        cos1, sin1 = turn(cut(1))
        exit_r = mid_r * cos1 - mid_i * sin1
        exit_i = mid_r * sin1 + mid_i * cos1
        far_r, far_i = both_sides(exit_r, exit_i, high, low, 0)
        misfit = far_r * far_r + far_i * far_i - meas_ref[p]
        scale = (4.0 * LOSS_WEIGHT) * misfit
        g_r, g_i = both_sides(scale * far_r, scale * far_i, high, low, 1)
        paste(1, SIGMA * (g_i * exit_r - g_r * exit_i))
        b_r = g_r * cos1 + g_i * sin1
        b_i = g_i * cos1 - g_r * sin1
        g_r, g_i = both_sides(b_r, b_i, high, low, 3)
        paste(0, SIGMA * (g_i * first_r - g_r * first_i))
        return carry

    lax.fori_loop(0, meas_ref.shape[0], probe, 0)


def probe_gradients(corners, extended, illumination, measured, interpret=False):
    high, low = block_tables(illumination.shape[1])
    vmem = pl.BlockSpec(memory_space=pltpu.VMEM)
    probes, width = measured.shape[0], measured.shape[1]
    flops = probes * 4 * 2 * 3 * 2 * (2 * width) ** 2 * width
    return pl.pallas_call(
        probes_kernel,
        out_shape=jax.ShapeDtypeStruct(extended.shape, jnp.float32),
        in_specs=[pl.BlockSpec(memory_space=pltpu.SMEM)] + [vmem] * 5,
        out_specs=vmem,
        compiler_params=pltpu.CompilerParams(vmem_limit_bytes=56 * 2**20),
        cost_estimate=pl.CostEstimate(flops=flops, bytes_accessed=16 * 2**20, transcendentals=0),
        interpret=interpret,
    )(corners, extended, illumination, measured, jnp.asarray(high), jnp.asarray(low))


def places():
    tile, owner = lax.axis_index("tile"), lax.axis_index("owner")
    partner = owner + 1 - 2 * (owner % 2)
    return tile, owner, partner, tile % TX != 0, tile % TX != TX - 1


def greet(owners):
    tile, owner, partner, has_left, has_right = places()
    barrier = pltpu.get_barrier_semaphore()

    def hello(device):
        pl.semaphore_signal(barrier, inc=1, device_id=device, device_id_type=MESH)

    hello({"owner": partner})
    for j in range(1, owners // 2):
        hello({"owner": (owner + 2 * j) % owners})
    pl.when(has_left)(lambda: hello({"tile": tile - 1}))
    pl.when(has_right)(lambda: hello({"tile": tile + 1}))
    beside = has_left.astype(jnp.int32) + has_right.astype(jnp.int32)
    pl.semaphore_wait(barrier, owners // 2 + beside)


def gather_kernel(owners, part_ref, ext_ref, send, recv):
    tile, owner, partner, has_left, has_right = places()
    layers, size, width = part_ref.shape
    chips = owners // 2
    peers = range(1, chips)

    def spot(s, who, side):
        start = pl.multiple_of(who * size, size)
        return ext_ref.at[s, pl.ds(start, size), pl.ds(side * width, width)]

    def copy(s, kind, src, dst, device):
        return pltpu.make_async_remote_copy(
            src_ref=src, dst_ref=dst, send_sem=send.at[s, kind], recv_sem=recv.at[s, kind],
            device_id=device, device_id_type=MESH,
        )

    def to_left(s):
        return copy(s, 0, part_ref.at[s], spot(s, owner, 1), {"tile": tile - 1})

    def to_partner(s, side):
        src = part_ref.at[s] if side == 0 else spot(s, owner, 1)
        return copy(s, 1 + side, src, spot(s, owner, side), {"owner": partner})

    def to_peer(s, side, j):
        src = part_ref.at[s] if side == 0 else spot(s, owner, 1)
        kind = 3 + side * (chips - 1) + j - 1
        return copy(s, kind, src, spot(s, owner, side), {"owner": (owner + 2 * j) % owners})

    def onward(s, side, j):
        block = spot(s, (owner + owners - 2 * j) % owners, side)
        kind = 3 + (2 + side) * (chips - 1) + j - 1
        return copy(s, kind, block, block, {"owner": partner})

    greet(owners)

    def spread(s, side):
        for j in peers:
            to_peer(s, side, j).start()
        to_partner(s, side).start()

    def pass_on(s, side):
        for j in peers:
            to_peer(s, side, j).wait_recv()
            onward(s, side, j).start()

    def finish(s, side):
        to_partner(s, side).wait()
        for j in peers:
            to_peer(s, side, j).wait_send()
            onward(s, side, j).wait()

    for s in range(layers):
        pl.when(has_left)(lambda s=s: to_left(s).start())
    spread(0, 0)
    for s in range(layers):
        @pl.when(has_right)
        def _(s=s):
            to_left(s).wait_recv()
            spread(s, 1)

        if s + 1 < layers:
            spread(s + 1, 0)
        ext_ref[s, pl.ds(pl.multiple_of(owner * size, size), size), :width] = part_ref[s]

        @pl.when(jnp.logical_not(has_right))
        def _(s=s):
            ext_ref[s, :, width:] = jnp.zeros((ext_ref.shape[1], width), ext_ref.dtype)

    for s in range(layers):
        pass_on(s, 0)
        pl.when(has_right)(lambda s=s: pass_on(s, 1))
    for s in range(layers):
        finish(s, 0)
        pl.when(has_right)(lambda s=s: finish(s, 1))
        pl.when(has_left)(lambda s=s: to_left(s).wait_send())


def gather_grid(rows_part):
    owners = lax.axis_size("owner")
    layers, size, width = rows_part.shape
    kinds = 3 + 4 * (owners // 2 - 1)
    vmem = pl.BlockSpec(memory_space=pltpu.VMEM)
    return pl.pallas_call(
        functools.partial(gather_kernel, owners),
        out_shape=jax.ShapeDtypeStruct((layers, owners * size, 2 * width), rows_part.dtype),
        in_specs=[vmem],
        out_specs=vmem,
        scratch_shapes=[pltpu.SemaphoreType.DMA((layers, kinds))] * 2,
        compiler_params=pltpu.CompilerParams(
            collective_id=0, has_side_effects=True, vmem_limit_bytes=56 * 2**20
        ),
    )(rows_part)


def reduce_kernel(owners, grad_ref, out_ref, near, total, far, edge, edge_in, sends, recvs):
    tile, owner, partner, has_left, has_right = places()
    layers, size, width = out_ref.shape
    chips = owners // 2
    order = [(s, side) for side in (1, 0) for s in range(layers)]

    def rows(who):
        return pl.ds(pl.multiple_of(who * size, size), size)

    def cols(side):
        return pl.ds(side * width, width)

    def to_partner(s, side, j):
        src = grad_ref.at[s, rows((partner + 2 * j) % owners), cols(side)]
        return pltpu.make_async_remote_copy(
            src_ref=src, dst_ref=near.at[s, side, j],
            send_sem=sends.at[s, side, j], recv_sem=recvs.at[s, side, j],
            device_id={"owner": partner}, device_id_type=MESH,
        )

    def to_peer(s, side, j):
        return pltpu.make_async_remote_copy(
            src_ref=total.at[s, side, j - 1], dst_ref=far.at[s, side, j - 1],
            send_sem=sends.at[s, side, chips + j - 1], recv_sem=recvs.at[s, side, chips + j - 1],
            device_id={"owner": (owner + 2 * j) % owners}, device_id_type=MESH,
        )

    def to_right(s):
        return pltpu.make_async_remote_copy(
            src_ref=edge.at[s], dst_ref=edge_in.at[s],
            send_sem=sends.at[s, 0, 2 * chips - 1], recv_sem=recvs.at[s, 0, 2 * chips - 1],
            device_id={"tile": tile + 1}, device_id_type=MESH,
        )

    greet(owners)
    peers = list(range(1, chips))
    for s, side in order:
        for j in peers + [0]:
            to_partner(s, side, j).start()
    for s, side in order:
        for j in peers:
            to_partner(s, side, j).wait_recv()
            own = grad_ref[s, rows((owner + 2 * j) % owners), cols(side)]
            total[s, side, j - 1] = own + near[s, side, j]
            to_peer(s, side, j).start()
    for s, side in order:
        to_partner(s, side, 0).wait_recv()
        value = grad_ref[s, rows(owner), cols(side)] + near[s, side, 0]
        for j in peers:
            to_peer(s, side, j).wait_recv()
            value = value + far[s, side, j - 1]
        if side == 1:
            edge[s] = value
            pl.when(has_right)(lambda s=s: to_right(s).start())
        else:
            out_ref[s] = value
    for s in range(layers):
        @pl.when(has_left)
        def _(s=s):
            to_right(s).wait_recv()
            out_ref[s] += edge_in[s]

    for s, side in order:
        for j in peers + [0]:
            to_partner(s, side, j).wait_send()
        for j in peers:
            to_peer(s, side, j).wait_send()
    for s in range(layers):
        pl.when(has_right)(lambda s=s: to_right(s).wait_send())


def reduce_grid(wide_grad):
    owners = lax.axis_size("owner")
    layers, tile_rows, cols = wide_grad.shape
    size, width, chips = tile_rows // owners, cols // 2, owners // 2
    vmem = pl.BlockSpec(memory_space=pltpu.VMEM)
    block = (size, width)
    return pl.pallas_call(
        functools.partial(reduce_kernel, owners),
        out_shape=jax.ShapeDtypeStruct((layers,) + block, jnp.float32),
        in_specs=[vmem],
        out_specs=vmem,
        scratch_shapes=[
            pltpu.VMEM((layers, 2, chips) + block, jnp.float32),
            pltpu.VMEM((layers, 2, max(chips - 1, 1)) + block, jnp.float32),
            pltpu.VMEM((layers, 2, max(chips - 1, 1)) + block, jnp.float32),
            pltpu.VMEM((layers,) + block, jnp.float32),
            pltpu.VMEM((layers,) + block, jnp.float32),
            pltpu.SemaphoreType.DMA((layers, 2, 2 * chips)),
            pltpu.SemaphoreType.DMA((layers, 2, 2 * chips)),
        ],
        compiler_params=pltpu.CompilerParams(
            collective_id=1, has_side_effects=True, vmem_limit_bytes=56 * 2**20
        ),
    )(wide_grad)


def encode(x):
    largest = jnp.maximum(jnp.max(jnp.abs(x), axis=0, keepdims=True), 1e-30)
    code = jnp.round(x * (32767.0 / largest)).astype(jnp.int32).astype(jnp.int16)
    return code, jnp.broadcast_to(largest * (1.0 / 32767.0), (8, x.shape[1]))


def decode(code, scale):
    return code.astype(jnp.int32).astype(jnp.float32) * scale[:1]


class Several:
    def __init__(self, *copies):
        self.copies = copies

    def start(self):
        for copy in self.copies:
            copy.start()

    def wait_send(self):
        for copy in self.copies:
            copy.wait_send()

    def wait_recv(self):
        for copy in self.copies:
            copy.wait_recv()


def fused_kernel(
    owners, place_ref, part_ref, illum_ref, meas_hbm, high_hbm, low_hbm, out_ref,
    ext0, ext1, meas_ref, high, low, first, back, pads, grad, near, total, far, edge, edge_in,
    total_scale, far_scale, edge_scale, edge_in_scale, loads, g_send, g_recv, sends, recvs,
):
    tile, owner, partner, has_left, has_right = places()
    layers, groups, _, width = part_ref.shape
    size = groups * ALIGN
    chips = owners // 2
    peers = list(range(1, chips))
    probes = meas_ref.shape[0]
    cols_all = 2 * width
    rows_all = owners * size
    span = width + ALIGN
    ext = (ext0, ext1)
    tail = width + 8

    fetches = [
        pltpu.make_async_copy(src, dst, loads.at[i])
        for i, (src, dst) in enumerate(((high_hbm, high), (low_hbm, low), (meas_hbm, meas_ref)))
    ]
    for fetch in fetches:
        fetch.start()
    greet(owners)

    def spot(s, who, side):
        return ext[s].at[pl.ds(who * groups, groups), :, pl.ds(side * width, width)]

    def g_copy(s, kind, src, dst, device):
        return pltpu.make_async_remote_copy(
            src_ref=src, dst_ref=dst, send_sem=g_send.at[s, kind], recv_sem=g_recv.at[s, kind],
            device_id=device, device_id_type=MESH,
        )

    def own(s, side):
        return part_ref.at[s] if side == 0 else spot(s, owner, 1)

    def g_left(s):
        return g_copy(s, 0, part_ref.at[s], spot(s, owner, 1), {"tile": tile - 1})

    def g_partner(s, side):
        return g_copy(s, 1 + side, own(s, side), spot(s, owner, side), {"owner": partner})

    def g_peer(s, side, j):
        kind = 3 + side * (chips - 1) + j - 1
        device = {"owner": (owner + 2 * j) % owners}
        return g_copy(s, kind, own(s, side), spot(s, owner, side), device)

    def g_onward(s, side, j):
        block = spot(s, (owner + owners - 2 * j) % owners, side)
        kind = 3 + (2 + side) * (chips - 1) + j - 1
        return g_copy(s, kind, block, block, {"owner": partner})

    def spread(s, side):
        for j in peers:
            g_peer(s, side, j).start()
        g_partner(s, side).start()

    def pass_on(s, side):
        for j in peers:
            g_peer(s, side, j).wait_recv()
            g_onward(s, side, j).start()

    def landed(s, side):
        g_partner(s, side).wait_recv()
        for j in peers:
            g_onward(s, side, j).wait_recv()

    def sent(s, side):
        g_partner(s, side).wait_send()
        for j in peers:
            g_peer(s, side, j).wait_send()
            g_onward(s, side, j).wait_send()

    def right_spread(s):
        g_left(s).wait_recv()
        spread(s, 1)

    for s in range(layers):
        pl.when(has_left)(lambda s=s: g_left(s).start())
    spread(0, 0)
    blank = jnp.zeros((probes, size // 8, 8, cols_all), jnp.float32)
    pads[:, : size // 8] = blank
    pads[:, (size + tail) // 8 :] = blank
    for s in range(layers):
        ext[s][pl.ds(owner * groups, groups), :, :width] = part_ref[s]

        @pl.when(jnp.logical_not(has_right))
        def _(s=s):
            ext[s][:, :, width:] = jnp.zeros((rows_all // ALIGN, ALIGN, width), part_ref.dtype)

    pl.when(has_right)(lambda: right_spread(0))
    spread(1, 0)
    pass_on(0, 0)
    pl.when(has_right)(lambda: pass_on(0, 1))
    pl.when(has_right)(lambda: right_spread(1))
    landed(0, 0)
    pl.when(has_right)(lambda: landed(0, 1))
    for fetch in fetches:
        fetch.wait()

    def pick(shape, dim, shift):
        along = lax.broadcasted_iota(jnp.int32, shape, dim)
        other = lax.broadcasted_iota(jnp.int32, shape, 1 - dim)
        return jnp.where(along == other + shift, 1.0, 0.0).astype(jnp.bfloat16)

    def dot(x, y):
        return jnp.dot(x, y, preferred_element_type=jnp.float32)

    def cut(s, p):
        base = place_ref[p, 0]
        x = jnp.concatenate([ext[s][base + i] for i in range(span // ALIGN)], axis=0)
        x = dot(x, pick((cols_all, width), 0, place_ref[p, 2])).astype(jnp.bfloat16)
        return dot(pick((width, span), 1, place_ref[p, 1]), x)

    def paste(p, g):
        down = pick((tail, width), 0, place_ref[p, 3])
        a, b = halves(g)
        a, b = halves(dot(down, a) + dot(down, b))
        along = pick((width, cols_all), 1, place_ref[p, 2])
        value = dot(a, along) + dot(b, along)
        pads[p, pl.ds(size // 8, tail // 8)] = value.reshape(tail // 8, 8, cols_all)

    def members(g):
        return [g * GROUP + k for k in range(GROUP)]

    def enter(g, carry):
        waves = []
        for p in members(g):
            cos0, sin0 = turn(cut(0, p))
            first[p, 0] = illum_ref[0] * cos0 - illum_ref[1] * sin0
            first[p, 1] = illum_ref[0] * sin0 + illum_ref[1] * cos0
            waves.append((first[p, 0], first[p, 1]))
        waves = both_sides_of(waves, high, low, 2)
        for p, (real, imag) in zip(members(g), waves):
            back[p, 0] = real
            back[p, 1] = imag
        return carry

    def forward(g, carry):
        turns, exits = [], []
        for p in members(g):
            cos1, sin1 = turn(cut(1, p))
            mid_r, mid_i = back[p, 0], back[p, 1]
            turns.append((cos1, sin1))
            exits.append((mid_r * cos1 - mid_i * sin1, mid_r * sin1 + mid_i * cos1))
        waves = []
        for p, (far_r, far_i) in zip(members(g), both_sides_of(exits, high, low, 0)):
            misfit = far_r * far_r + far_i * far_i - meas_ref[p]
            scale = (4.0 * LOSS_WEIGHT) * misfit
            waves.append((scale * far_r, scale * far_i))
        waves = both_sides_of(waves, high, low, 1)
        for p, (g_r, g_i), (cos1, sin1), (exit_r, exit_i) in zip(members(g), waves, turns, exits):
            back[p, 0] = g_r * cos1 + g_i * sin1
            back[p, 1] = g_i * cos1 - g_r * sin1
            paste(p, SIGMA * (g_i * exit_r - g_r * exit_i))
        return carry

    def backward(g, carry):
        waves = both_sides_of([(back[p, 0], back[p, 1]) for p in members(g)], high, low, 3)
        for p, (g_r, g_i) in zip(members(g), waves):
            paste(p, SIGMA * (g_i * first[p, 0] - g_r * first[p, 1]))
        return carry

    def rows(who):
        return pl.ds(pl.multiple_of(who * size, size), size)

    def cols(side):
        return pl.ds(side * width, width)

    def r_copy(s, kind, src, dst, device):
        return pltpu.make_async_remote_copy(
            src_ref=src, dst_ref=dst, send_sem=sends.at[s, kind], recv_sem=recvs.at[s, kind],
            device_id=device, device_id_type=MESH,
        )

    def to_partner(s, side, j):
        src = grad.at[s, rows((partner + 2 * j) % owners), cols(side)]
        return r_copy(s, side * chips + j, src, near.at[s, side, j], {"owner": partner})

    def to_peer(s, side, j):
        kind = 2 * chips + side * (chips - 1) + j - 1
        device = {"owner": (owner + 2 * j) % owners}
        at = (s, side, j - 1)
        more = kind + 2 * chips - 1
        return Several(
            r_copy(s, kind, total.at[at], far.at[at], device),
            r_copy(s, more, total_scale.at[at], far_scale.at[at], device),
        )

    def to_right(s):
        device = {"tile": tile + 1}
        return Several(
            r_copy(s, 4 * chips - 2, edge.at[s], edge_in.at[s], device),
            r_copy(s, 6 * chips - 3, edge_scale.at[s], edge_in_scale.at[s], device),
        )

    def block_sum(who, side):
        starts = [place_ref[p, 4 + who] for p in range(probes)]
        parts = []
        for i in range(size // 8):
            terms = [pads[p, starts[p] + i, :, cols(side)] for p in range(probes)]
            parts.append(functools.reduce(jnp.add, terms))
        value = jnp.concatenate(parts, axis=0)
        return value

    def give(s):
        for side in (1, 0):
            for j in peers + [0]:
                who = (partner + 2 * j) % owners
                grad[s, rows(who), cols(side)] = block_sum(who, side)
                to_partner(s, side, j).start()
        for side in (1, 0):
            for j in peers + [0]:
                who = (owner + 2 * j) % owners
                grad[s, rows(who), cols(side)] = block_sum(who, side)

    def across(s):
        for side in (1, 0):
            for j in peers:
                to_partner(s, side, j).wait_recv()
                mine = grad[s, rows((owner + 2 * j) % owners), cols(side)]
                code, scale = encode(mine + near[s, side, j])
                total[s, side, j - 1] = code
                total_scale[s, side, j - 1] = scale
                to_peer(s, side, j).start()

    def collect(s, side):
        to_partner(s, side, 0).wait_recv()
        value = grad[s, rows(owner), cols(side)] + near[s, side, 0]
        for j in peers:
            to_peer(s, side, j).wait_recv()
            value = value + decode(far[s, side, j - 1], far_scale[s, side, j - 1])
        if side == 1:
            edge[s], edge_scale[s] = encode(value)
            pl.when(has_right)(lambda: to_right(s).start())
        else:
            out_ref[s] = value

    def add_edge(s):
        to_right(s).wait_recv()
        out_ref[s] += decode(edge_in[s], edge_in_scale[s])

    groups_all = probes // GROUP
    lax.fori_loop(0, 1, enter, 0)
    pass_on(1, 0)
    pl.when(has_right)(lambda: pass_on(1, 1))
    lax.fori_loop(1, groups_all, enter, 0)
    landed(1, 0)
    pl.when(has_right)(lambda: landed(1, 1))
    lax.fori_loop(0, groups_all, forward, 0)
    give(1)
    lax.fori_loop(0, 1, backward, 0)
    across(1)
    lax.fori_loop(1, groups_all, backward, 0)
    collect(1, 1)
    give(0)
    across(0)
    collect(1, 0)
    collect(0, 1)
    collect(0, 0)
    for s in (1, 0):
        pl.when(has_left)(lambda s=s: add_edge(s))

    for s in range(layers):
        sent(s, 0)
        pl.when(has_right)(lambda s=s: sent(s, 1))
        pl.when(has_left)(lambda s=s: g_left(s).wait_send())
        for side in (0, 1):
            for j in peers + [0]:
                to_partner(s, side, j).wait_send()
            for j in peers:
                to_peer(s, side, j).wait_send()
        pl.when(has_right)(lambda s=s: to_right(s).wait_send())


def fused(rows_part, positions, illumination, measured):
    owners = lax.axis_size("owner")
    layers, size, width = rows_part.shape
    probes = measured.shape[0]
    chips = owners // 2
    peers = max(chips - 1, 1)
    high, low = block_tables(width)
    tile = lax.axis_index("tile")
    row = positions[:, 0] - tile // TX * (owners * size)
    col = positions[:, 1] - tile % TX * width
    base = jnp.minimum(row // ALIGN * ALIGN, owners * size - width - ALIGN)
    starts = size + jnp.arange(owners)[None, :] * size - (row // 8 * 8)[:, None]
    starts = jnp.clip(starts, 0, size + width + 8)
    heads = jnp.stack([base // ALIGN, row - base, col, row % 8], axis=1)
    place = jnp.concatenate([heads, starts // 8], axis=1)
    place = place.astype(jnp.int32)
    grouped = rows_part.reshape(layers, size // ALIGN, ALIGN, width)
    vmem = pl.BlockSpec(memory_space=pltpu.VMEM)
    anywhere = pl.BlockSpec(memory_space=pl.ANY)
    block = (size, width)
    f32 = jnp.float32
    flops = probes * 4 * 2 * 3 * 2 * (2 * width) ** 2 * width
    return pl.pallas_call(
        functools.partial(fused_kernel, owners),
        out_shape=jax.ShapeDtypeStruct((layers,) + block, f32),
        in_specs=[pl.BlockSpec(memory_space=pltpu.SMEM), vmem, vmem] + [anywhere] * 3,
        out_specs=vmem,
        scratch_shapes=[
            pltpu.VMEM((owners * size // ALIGN, ALIGN, 2 * width), rows_part.dtype),
            pltpu.VMEM((owners * size // ALIGN, ALIGN, 2 * width), rows_part.dtype),
            pltpu.VMEM(measured.shape, f32),
            pltpu.VMEM(high.shape, jnp.bfloat16),
            pltpu.VMEM(low.shape, jnp.bfloat16),
            pltpu.VMEM((probes, 2, width, width), f32),
            pltpu.VMEM((probes, 2, width, width), f32),
            pltpu.VMEM((probes, (2 * size + width) // 8 + 1, 8, 2 * width), f32),
            pltpu.VMEM((layers, owners * size, 2 * width), f32),
            pltpu.VMEM((layers, 2, chips) + block, f32),
            pltpu.VMEM((layers, 2, peers) + block, jnp.int16),
            pltpu.VMEM((layers, 2, peers) + block, jnp.int16),
            pltpu.VMEM((layers,) + block, jnp.int16),
            pltpu.VMEM((layers,) + block, jnp.int16),
            pltpu.VMEM((layers, 2, peers, 8, width), f32),
            pltpu.VMEM((layers, 2, peers, 8, width), f32),
            pltpu.VMEM((layers, 8, width), f32),
            pltpu.VMEM((layers, 8, width), f32),
            pltpu.SemaphoreType.DMA((3,)),
            pltpu.SemaphoreType.DMA((layers, 3 + 4 * (chips - 1))),
            pltpu.SemaphoreType.DMA((layers, 3 + 4 * (chips - 1))),
            pltpu.SemaphoreType.DMA((layers, 6 * chips - 2)),
            pltpu.SemaphoreType.DMA((layers, 6 * chips - 2)),
        ],
        compiler_params=pltpu.CompilerParams(
            collective_id=2, has_side_effects=True, vmem_limit_bytes=56 * 2**20
        ),
        cost_estimate=pl.CostEstimate(flops=flops, bytes_accessed=8 * 2**20, transcendentals=0),
    )(place, grouped, illumination, measured, jnp.asarray(high), jnp.asarray(low))


def body(potential, positions, illumination, measured):
    probe_width = illumination.shape[1]
    rows_part = potential[:, 0]
    layers = rows_part.shape[0]
    tile_rows = rows_part.shape[1] * lax.axis_size("owner")
    tile_cols = rows_part.shape[2]
    below = lax.axis_size("tile") > TX
    if not below and layers == 2 and measured.shape[0] % GROUP == 0:
        return fused(rows_part, positions, illumination, measured)[:, None]
    extended = gather_grid(rows_part)
    if below:
        lower_rim = passed_along(extended[:, :probe_width, :], "tile", -TX)
        extended = jnp.concatenate([extended, lower_rim], axis=1)
    tile_id = lax.axis_index("tile")
    first = jnp.stack([tile_id // TX * tile_rows, tile_id % TX * tile_cols])
    corners = positions - first[None, :].astype(jnp.int32)
    accumulated = probe_gradients(corners, extended, illumination, measured)
    wide_grad = accumulated[:, :tile_rows, :]
    if below:
        upper_back = passed_along(accumulated[:, tile_rows:, :], "tile", TX)
        wide_grad = wide_grad.at[:, :probe_width, :].add(upper_back)
    return reduce_grid(wide_grad)[:, None]


def solution(mesh):
    in_specs = (
        P(None, "tile", "owner", None),
        P(("tile", "owner"), None),
        P(),
        P(("tile", "owner"), None, None),
    )
    out_specs = P(None, "tile", "owner", None)
    return jax.shard_map(body, mesh=mesh, in_specs=in_specs, out_specs=out_specs, check_vma=False)
```

```python
import functools
import math

import jax
import jax.numpy as jnp
import numpy as np
from jax import lax
from jax.experimental import pallas as pl
from jax.experimental.pallas import tpu as pltpu
from jax.sharding import PartitionSpec as P

TX = 8

SIGMA = 0.5
LOSS_WEIGHT = 0.125
ALIGN = 16
GROUP = 2
MESH = pl.DeviceIdType.MESH


def passed_along(block, axis, distance):
    devices = range(lax.axis_size(axis))
    route = [(i - distance, i) for i in devices if i - distance in devices]
    return lax.ppermute(block, axis, route)


def block_tables(width):
    counter = np.arange(width)
    signed = (counter + width // 2) % width - width // 2
    angle = 2.0 * np.pi / width * (counter[:, None] * counter[None, :] % width)
    dft = np.exp(-1j * angle) / math.sqrt(width)
    chirp = np.exp(-4j * np.pi * signed.astype(np.float64) ** 2 / (width * width))
    prop = (np.conj(dft) * chirp[None, :]) @ dft

    def right(m):
        return np.block([[m.real, m.imag], [-m.imag, m.real]])

    full = np.stack([right(dft), right(np.conj(dft)), right(prop), right(np.conj(prop))])
    full = full.astype(np.float32)
    high = full.astype(jnp.bfloat16)
    low = (full - high.astype(np.float32)).astype(jnp.bfloat16)
    return high, low


def halves(x):
    high = x.astype(jnp.bfloat16)
    low = (x - high.astype(jnp.float32)).astype(jnp.bfloat16)
    return high, low


def dot3(a, b):
    def dot(x, y):
        return jnp.dot(x, y, preferred_element_type=jnp.float32)

    return dot(a[0], b[0]) + (dot(a[0], b[1]) + dot(a[1], b[0]))


def both_sides(real, imag, high, low, which):
    width = real.shape[0]
    wide = jnp.concatenate([real, imag], axis=1)
    wide = dot3(halves(wide), (high[which], low[which]))
    tall = jnp.concatenate([wide[:, :width], wide[:, width:]], axis=0)
    other = which ^ 1
    tall = dot3((high[other], low[other]), halves(tall))
    return tall[:width], tall[width:]


def triple_tables(width):
    high, low = block_tables(width)
    right = np.concatenate([high, high, low], axis=1)
    left = np.concatenate([high, low, high], axis=2)
    return jnp.asarray(right), jnp.asarray(left)


def both_sides_of(waves, right, left, which):
    width = waves[0][0].shape[0]

    def dot(x, y):
        return jnp.dot(x, y, preferred_element_type=jnp.float32)

    wide = jnp.concatenate([jnp.concatenate(wave, axis=1) for wave in waves], axis=0)
    a, b = halves(wide)
    wide = dot(jnp.concatenate([a, b, a], axis=1), right[which])
    spans = [slice(k * width, (k + 1) * width) for k in range(len(waves))]
    real = jnp.concatenate([wide[span, :width] for span in spans], axis=1)
    imag = jnp.concatenate([wide[span, width:] for span in spans], axis=1)
    a, b = halves(jnp.concatenate([real, imag], axis=0))
    tall = dot(left[which ^ 1], jnp.concatenate([a, a, b], axis=0))
    return [(tall[:width, span], tall[width:, span]) for span in spans]


def turn(window):
    y = (0.5 * SIGMA) * window
    z = y * y
    sine = -1.0 / 39916800.0
    for c in (1.0 / 362880.0, -1.0 / 5040.0, 1.0 / 120.0, -1.0 / 6.0, 1.0):
        sine = sine * z + c
    sine = sine * y
    cosine = 1.0 / 479001600.0
    for c in (-1.0 / 3628800.0, 1.0 / 40320.0, -1.0 / 720.0, 1.0 / 24.0, -0.5, 1.0):
        cosine = cosine * z + c
    return 1.0 - 2.0 * sine * sine, 2.0 * sine * cosine


def probes_kernel(corner_ref, ext_ref, illum_ref, meas_ref, high, low, acc_ref):
    width = illum_ref.shape[1]
    rows, cols = ext_ref.shape[1], ext_ref.shape[2]
    span = width + ALIGN
    acc_ref[...] = jnp.zeros_like(acc_ref)

    def probe(p, carry):
        r = corner_ref[p, 0]
        c = corner_ref[p, 1]
        base = pl.multiple_of(jnp.minimum((r // ALIGN) * ALIGN, rows - span), ALIGN)
        shift = r - base

        def cut(s):
            x = ext_ref[s, pl.ds(base, span), :].astype(jnp.float32)
            x = pltpu.roll(x, span - shift, 0)[:width]
            return pltpu.roll(x, cols - c, 1)[:, :width]

        def paste(s, g):
            x = jnp.concatenate([g, jnp.zeros((width, cols - width), jnp.float32)], axis=1)
            x = pltpu.roll(x, c, 1)
            x = jnp.concatenate([x, jnp.zeros((ALIGN, cols), jnp.float32)], axis=0)
            acc_ref[s, pl.ds(base, span), :] += pltpu.roll(x, shift, 0)

        cos0, sin0 = turn(cut(0))
        first_r = illum_ref[0] * cos0 - illum_ref[1] * sin0
        first_i = illum_ref[0] * sin0 + illum_ref[1] * cos0
        mid_r, mid_i = both_sides(first_r, first_i, high, low, 2)
        cos1, sin1 = turn(cut(1))
        exit_r = mid_r * cos1 - mid_i * sin1
        exit_i = mid_r * sin1 + mid_i * cos1
        far_r, far_i = both_sides(exit_r, exit_i, high, low, 0)
        misfit = far_r * far_r + far_i * far_i - meas_ref[p]
        scale = (4.0 * LOSS_WEIGHT) * misfit
        g_r, g_i = both_sides(scale * far_r, scale * far_i, high, low, 1)
        paste(1, SIGMA * (g_i * exit_r - g_r * exit_i))
        b_r = g_r * cos1 + g_i * sin1
        b_i = g_i * cos1 - g_r * sin1
        g_r, g_i = both_sides(b_r, b_i, high, low, 3)
        paste(0, SIGMA * (g_i * first_r - g_r * first_i))
        return carry

    lax.fori_loop(0, meas_ref.shape[0], probe, 0)


def probe_gradients(corners, extended, illumination, measured, interpret=False):
    high, low = block_tables(illumination.shape[1])
    vmem = pl.BlockSpec(memory_space=pltpu.VMEM)
    probes, width = measured.shape[0], measured.shape[1]
    flops = probes * 4 * 2 * 3 * 2 * (2 * width) ** 2 * width
    return pl.pallas_call(
        probes_kernel,
        out_shape=jax.ShapeDtypeStruct(extended.shape, jnp.float32),
        in_specs=[pl.BlockSpec(memory_space=pltpu.SMEM)] + [vmem] * 5,
        out_specs=vmem,
        compiler_params=pltpu.CompilerParams(vmem_limit_bytes=56 * 2**20),
        cost_estimate=pl.CostEstimate(flops=flops, bytes_accessed=16 * 2**20, transcendentals=0),
        interpret=interpret,
    )(corners, extended, illumination, measured, jnp.asarray(high), jnp.asarray(low))


def places():
    tile, owner = lax.axis_index("tile"), lax.axis_index("owner")
    partner = owner + 1 - 2 * (owner % 2)
    return tile, owner, partner, tile % TX != 0, tile % TX != TX - 1


def greet(owners):
    tile, owner, partner, has_left, has_right = places()
    barrier = pltpu.get_barrier_semaphore()

    def hello(device):
        pl.semaphore_signal(barrier, inc=1, device_id=device, device_id_type=MESH)

    hello({"owner": partner})
    for j in range(1, owners // 2):
        hello({"owner": (owner + 2 * j) % owners})
    pl.when(has_left)(lambda: hello({"tile": tile - 1}))
    pl.when(has_right)(lambda: hello({"tile": tile + 1}))
    beside = has_left.astype(jnp.int32) + has_right.astype(jnp.int32)
    pl.semaphore_wait(barrier, owners // 2 + beside)


def gather_kernel(owners, part_ref, ext_ref, send, recv):
    tile, owner, partner, has_left, has_right = places()
    layers, size, width = part_ref.shape
    chips = owners // 2
    peers = range(1, chips)

    def spot(s, who, side):
        start = pl.multiple_of(who * size, size)
        return ext_ref.at[s, pl.ds(start, size), pl.ds(side * width, width)]

    def copy(s, kind, src, dst, device):
        return pltpu.make_async_remote_copy(
            src_ref=src, dst_ref=dst, send_sem=send.at[s, kind], recv_sem=recv.at[s, kind],
            device_id=device, device_id_type=MESH,
        )

    def to_left(s):
        return copy(s, 0, part_ref.at[s], spot(s, owner, 1), {"tile": tile - 1})

    def to_partner(s, side):
        src = part_ref.at[s] if side == 0 else spot(s, owner, 1)
        return copy(s, 1 + side, src, spot(s, owner, side), {"owner": partner})

    def to_peer(s, side, j):
        src = part_ref.at[s] if side == 0 else spot(s, owner, 1)
        kind = 3 + side * (chips - 1) + j - 1
        return copy(s, kind, src, spot(s, owner, side), {"owner": (owner + 2 * j) % owners})

    def onward(s, side, j):
        block = spot(s, (owner + owners - 2 * j) % owners, side)
        kind = 3 + (2 + side) * (chips - 1) + j - 1
        return copy(s, kind, block, block, {"owner": partner})

    greet(owners)

    def spread(s, side):
        for j in peers:
            to_peer(s, side, j).start()
        to_partner(s, side).start()

    def pass_on(s, side):
        for j in peers:
            to_peer(s, side, j).wait_recv()
            onward(s, side, j).start()

    def finish(s, side):
        to_partner(s, side).wait()
        for j in peers:
            to_peer(s, side, j).wait_send()
            onward(s, side, j).wait()

    for s in range(layers):
        pl.when(has_left)(lambda s=s: to_left(s).start())
    spread(0, 0)
    for s in range(layers):
        @pl.when(has_right)
        def _(s=s):
            to_left(s).wait_recv()
            spread(s, 1)

        if s + 1 < layers:
            spread(s + 1, 0)
        ext_ref[s, pl.ds(pl.multiple_of(owner * size, size), size), :width] = part_ref[s]

        @pl.when(jnp.logical_not(has_right))
        def _(s=s):
            ext_ref[s, :, width:] = jnp.zeros((ext_ref.shape[1], width), ext_ref.dtype)

    for s in range(layers):
        pass_on(s, 0)
        pl.when(has_right)(lambda s=s: pass_on(s, 1))
    for s in range(layers):
        finish(s, 0)
        pl.when(has_right)(lambda s=s: finish(s, 1))
        pl.when(has_left)(lambda s=s: to_left(s).wait_send())


def gather_grid(rows_part):
    owners = lax.axis_size("owner")
    layers, size, width = rows_part.shape
    kinds = 3 + 4 * (owners // 2 - 1)
    vmem = pl.BlockSpec(memory_space=pltpu.VMEM)
    return pl.pallas_call(
        functools.partial(gather_kernel, owners),
        out_shape=jax.ShapeDtypeStruct((layers, owners * size, 2 * width), rows_part.dtype),
        in_specs=[vmem],
        out_specs=vmem,
        scratch_shapes=[pltpu.SemaphoreType.DMA((layers, kinds))] * 2,
        compiler_params=pltpu.CompilerParams(
            collective_id=0, has_side_effects=True, vmem_limit_bytes=56 * 2**20
        ),
    )(rows_part)


def reduce_kernel(owners, grad_ref, out_ref, near, total, far, edge, edge_in, sends, recvs):
    tile, owner, partner, has_left, has_right = places()
    layers, size, width = out_ref.shape
    chips = owners // 2
    order = [(s, side) for side in (1, 0) for s in range(layers)]

    def rows(who):
        return pl.ds(pl.multiple_of(who * size, size), size)

    def cols(side):
        return pl.ds(side * width, width)

    def to_partner(s, side, j):
        src = grad_ref.at[s, rows((partner + 2 * j) % owners), cols(side)]
        return pltpu.make_async_remote_copy(
            src_ref=src, dst_ref=near.at[s, side, j],
            send_sem=sends.at[s, side, j], recv_sem=recvs.at[s, side, j],
            device_id={"owner": partner}, device_id_type=MESH,
        )

    def to_peer(s, side, j):
        return pltpu.make_async_remote_copy(
            src_ref=total.at[s, side, j - 1], dst_ref=far.at[s, side, j - 1],
            send_sem=sends.at[s, side, chips + j - 1], recv_sem=recvs.at[s, side, chips + j - 1],
            device_id={"owner": (owner + 2 * j) % owners}, device_id_type=MESH,
        )

    def to_right(s):
        return pltpu.make_async_remote_copy(
            src_ref=edge.at[s], dst_ref=edge_in.at[s],
            send_sem=sends.at[s, 0, 2 * chips - 1], recv_sem=recvs.at[s, 0, 2 * chips - 1],
            device_id={"tile": tile + 1}, device_id_type=MESH,
        )

    greet(owners)
    peers = list(range(1, chips))
    for s, side in order:
        for j in peers + [0]:
            to_partner(s, side, j).start()
    for s, side in order:
        for j in peers:
            to_partner(s, side, j).wait_recv()
            own = grad_ref[s, rows((owner + 2 * j) % owners), cols(side)]
            total[s, side, j - 1] = own + near[s, side, j]
            to_peer(s, side, j).start()
    for s, side in order:
        to_partner(s, side, 0).wait_recv()
        value = grad_ref[s, rows(owner), cols(side)] + near[s, side, 0]
        for j in peers:
            to_peer(s, side, j).wait_recv()
            value = value + far[s, side, j - 1]
        if side == 1:
            edge[s] = value
            pl.when(has_right)(lambda s=s: to_right(s).start())
        else:
            out_ref[s] = value
    for s in range(layers):
        @pl.when(has_left)
        def _(s=s):
            to_right(s).wait_recv()
            out_ref[s] += edge_in[s]

    for s, side in order:
        for j in peers + [0]:
            to_partner(s, side, j).wait_send()
        for j in peers:
            to_peer(s, side, j).wait_send()
    for s in range(layers):
        pl.when(has_right)(lambda s=s: to_right(s).wait_send())


def reduce_grid(wide_grad):
    owners = lax.axis_size("owner")
    layers, tile_rows, cols = wide_grad.shape
    size, width, chips = tile_rows // owners, cols // 2, owners // 2
    vmem = pl.BlockSpec(memory_space=pltpu.VMEM)
    block = (size, width)
    return pl.pallas_call(
        functools.partial(reduce_kernel, owners),
        out_shape=jax.ShapeDtypeStruct((layers,) + block, jnp.float32),
        in_specs=[vmem],
        out_specs=vmem,
        scratch_shapes=[
            pltpu.VMEM((layers, 2, chips) + block, jnp.float32),
            pltpu.VMEM((layers, 2, max(chips - 1, 1)) + block, jnp.float32),
            pltpu.VMEM((layers, 2, max(chips - 1, 1)) + block, jnp.float32),
            pltpu.VMEM((layers,) + block, jnp.float32),
            pltpu.VMEM((layers,) + block, jnp.float32),
            pltpu.SemaphoreType.DMA((layers, 2, 2 * chips)),
            pltpu.SemaphoreType.DMA((layers, 2, 2 * chips)),
        ],
        compiler_params=pltpu.CompilerParams(
            collective_id=1, has_side_effects=True, vmem_limit_bytes=56 * 2**20
        ),
    )(wide_grad)


def encode(x):
    largest = jnp.maximum(jnp.max(jnp.abs(x), axis=0, keepdims=True), 1e-30)
    code = jnp.round(x * (32767.0 / largest)).astype(jnp.int32).astype(jnp.int16)
    return code, jnp.broadcast_to(largest * (1.0 / 32767.0), (8, x.shape[1]))


def decode(code, scale):
    return code.astype(jnp.int32).astype(jnp.float32) * scale[:1]


class Several:
    def __init__(self, *copies):
        self.copies = copies

    def start(self):
        for copy in self.copies:
            copy.start()

    def wait_send(self):
        for copy in self.copies:
            copy.wait_send()

    def wait_recv(self):
        for copy in self.copies:
            copy.wait_recv()


def fused_kernel(
    owners, place_ref, part_ref, illum_ref, meas_hbm, right_hbm, left_hbm, out_ref,
    ext0, ext1, meas_ref, right, left, first, back, pads, grad, near, total, far, edge, edge_in,
    total_scale, far_scale, edge_scale, edge_in_scale, loads, g_send, g_recv, sends, recvs,
):
    tile, owner, partner, has_left, has_right = places()
    layers, groups, _, width = part_ref.shape
    size = groups * ALIGN
    chips = owners // 2
    peers = list(range(1, chips))
    probes = meas_ref.shape[0]
    cols_all = 2 * width
    rows_all = owners * size
    span = width + ALIGN
    ext = (ext0, ext1)
    tail = width + 8

    fetches = [
        pltpu.make_async_copy(src, dst, loads.at[i])
        for i, (src, dst) in enumerate(((right_hbm, right), (left_hbm, left), (meas_hbm, meas_ref)))
    ]
    for fetch in fetches:
        fetch.start()
    greet(owners)

    def spot(s, who, side):
        return ext[s].at[pl.ds(who * groups, groups), :, pl.ds(side * width, width)]

    def g_copy(s, kind, src, dst, device):
        return pltpu.make_async_remote_copy(
            src_ref=src, dst_ref=dst, send_sem=g_send.at[s, kind], recv_sem=g_recv.at[s, kind],
            device_id=device, device_id_type=MESH,
        )

    def own(s, side):
        return part_ref.at[s] if side == 0 else spot(s, owner, 1)

    def g_left(s):
        return g_copy(s, 0, part_ref.at[s], spot(s, owner, 1), {"tile": tile - 1})

    def g_partner(s, side):
        return g_copy(s, 1 + side, own(s, side), spot(s, owner, side), {"owner": partner})

    def g_peer(s, side, j):
        kind = 3 + side * (chips - 1) + j - 1
        device = {"owner": (owner + 2 * j) % owners}
        return g_copy(s, kind, own(s, side), spot(s, owner, side), device)

    def g_onward(s, side, j):
        block = spot(s, (owner + owners - 2 * j) % owners, side)
        kind = 3 + (2 + side) * (chips - 1) + j - 1
        return g_copy(s, kind, block, block, {"owner": partner})

    def spread(s, side):
        for j in peers:
            g_peer(s, side, j).start()
        g_partner(s, side).start()

    def pass_on(s, side):
        for j in peers:
            g_peer(s, side, j).wait_recv()
            g_onward(s, side, j).start()

    def landed(s, side):
        g_partner(s, side).wait_recv()
        for j in peers:
            g_onward(s, side, j).wait_recv()

    def sent(s, side):
        g_partner(s, side).wait_send()
        for j in peers:
            g_peer(s, side, j).wait_send()
            g_onward(s, side, j).wait_send()

    def right_spread(s):
        g_left(s).wait_recv()
        spread(s, 1)

    pl.when(has_left)(lambda: g_left(0).start())
    spread(0, 0)
    blank = jnp.zeros((probes, size // 8, 8, cols_all), jnp.float32)
    pads[:, : size // 8] = blank
    pads[:, (size + tail) // 8 :] = blank
    for s in range(layers):
        ext[s][pl.ds(owner * groups, groups), :, :width] = part_ref[s]

        @pl.when(jnp.logical_not(has_right))
        def _(s=s):
            ext[s][:, :, width:] = jnp.zeros((rows_all // ALIGN, ALIGN, width), part_ref.dtype)

    pl.when(has_right)(lambda: right_spread(0))
    pl.when(has_left)(lambda: g_left(1).start())
    spread(1, 0)
    pass_on(0, 0)
    pl.when(has_right)(lambda: pass_on(0, 1))
    landed(0, 0)
    pl.when(has_right)(lambda: landed(0, 1))
    pl.when(has_right)(lambda: right_spread(1))
    for fetch in fetches:
        fetch.wait()

    def pick(shape, dim, shift):
        along = lax.broadcasted_iota(jnp.int32, shape, dim)
        other = lax.broadcasted_iota(jnp.int32, shape, 1 - dim)
        return jnp.where(along == other + shift, 1.0, 0.0).astype(jnp.bfloat16)

    def dot(x, y):
        return jnp.dot(x, y, preferred_element_type=jnp.float32)

    def cut(s, p):
        base = place_ref[p, 0]
        x = jnp.concatenate([ext[s][base + i] for i in range(span // ALIGN)], axis=0)
        x = dot(x, pick((cols_all, width), 0, place_ref[p, 2])).astype(jnp.bfloat16)
        return dot(pick((width, span), 1, place_ref[p, 1]), x)

    def paste(p, g):
        down = pick((tail, width), 0, place_ref[p, 3])
        a, b = halves(g)
        a, b = halves(dot(down, a) + dot(down, b))
        along = pick((width, cols_all), 1, place_ref[p, 2])
        value = dot(a, along) + dot(b, along)
        pads[p, pl.ds(size // 8, tail // 8)] = value.reshape(tail // 8, 8, cols_all)

    def members(g):
        return [g * GROUP + k for k in range(GROUP)]

    def enter(g, carry):
        waves = []
        for p in members(g):
            cos0, sin0 = turn(cut(0, p))
            first[p, 0] = illum_ref[0] * cos0 - illum_ref[1] * sin0
            first[p, 1] = illum_ref[0] * sin0 + illum_ref[1] * cos0
            waves.append((first[p, 0], first[p, 1]))
        waves = both_sides_of(waves, right, left, 2)
        for p, (real, imag) in zip(members(g), waves):
            back[p, 0] = real
            back[p, 1] = imag
        return carry

    def forward(g, carry):
        turns, exits = [], []
        for p in members(g):
            cos1, sin1 = turn(cut(1, p))
            mid_r, mid_i = back[p, 0], back[p, 1]
            turns.append((cos1, sin1))
            exits.append((mid_r * cos1 - mid_i * sin1, mid_r * sin1 + mid_i * cos1))
        waves = []
        for p, (far_r, far_i) in zip(members(g), both_sides_of(exits, right, left, 0)):
            misfit = far_r * far_r + far_i * far_i - meas_ref[p]
            scale = (4.0 * LOSS_WEIGHT) * misfit
            waves.append((scale * far_r, scale * far_i))
        waves = both_sides_of(waves, right, left, 1)
        for p, (g_r, g_i), (cos1, sin1), (exit_r, exit_i) in zip(members(g), waves, turns, exits):
            back[p, 0] = g_r * cos1 + g_i * sin1
            back[p, 1] = g_i * cos1 - g_r * sin1
            paste(p, SIGMA * (g_i * exit_r - g_r * exit_i))
        return carry

    def backward(g, carry):
        waves = both_sides_of([(back[p, 0], back[p, 1]) for p in members(g)], right, left, 3)
        for p, (g_r, g_i) in zip(members(g), waves):
            paste(p, SIGMA * (g_i * first[p, 0] - g_r * first[p, 1]))
        return carry

    def rows(who):
        return pl.ds(pl.multiple_of(who * size, size), size)

    def cols(side):
        return pl.ds(side * width, width)

    def r_copy(s, kind, src, dst, device):
        return pltpu.make_async_remote_copy(
            src_ref=src, dst_ref=dst, send_sem=sends.at[s, kind], recv_sem=recvs.at[s, kind],
            device_id=device, device_id_type=MESH,
        )

    def to_partner(s, side, j):
        src = grad.at[s, rows((partner + 2 * j) % owners), cols(side)]
        return r_copy(s, side * chips + j, src, near.at[s, side, j], {"owner": partner})

    def to_peer(s, side, j):
        kind = 2 * chips + side * (chips - 1) + j - 1
        device = {"owner": (owner + 2 * j) % owners}
        at = (s, side, j - 1)
        more = kind + 2 * chips - 1
        return Several(
            r_copy(s, kind, total.at[at], far.at[at], device),
            r_copy(s, more, total_scale.at[at], far_scale.at[at], device),
        )

    def to_right(s):
        device = {"tile": tile + 1}
        return Several(
            r_copy(s, 4 * chips - 2, edge.at[s], edge_in.at[s], device),
            r_copy(s, 6 * chips - 3, edge_scale.at[s], edge_in_scale.at[s], device),
        )

    def block_sum(who, side):
        starts = [place_ref[p, 4 + who] for p in range(probes)]
        parts = []
        for i in range(size // 8):
            terms = [pads[p, starts[p] + i, :, cols(side)] for p in range(probes)]
            parts.append(functools.reduce(jnp.add, terms))
        value = jnp.concatenate(parts, axis=0)
        return value

    def give(s):
        for side in (1, 0):
            for j in peers + [0]:
                who = (partner + 2 * j) % owners
                grad[s, rows(who), cols(side)] = block_sum(who, side)
                to_partner(s, side, j).start()
        for side in (1, 0):
            for j in peers + [0]:
                who = (owner + 2 * j) % owners
                grad[s, rows(who), cols(side)] = block_sum(who, side)

    def across(s):
        for side in (1, 0):
            for j in peers:
                to_partner(s, side, j).wait_recv()
                mine = grad[s, rows((owner + 2 * j) % owners), cols(side)]
                code, scale = encode(mine + near[s, side, j])
                total[s, side, j - 1] = code
                total_scale[s, side, j - 1] = scale
                to_peer(s, side, j).start()

    def collect(s, side):
        to_partner(s, side, 0).wait_recv()
        value = grad[s, rows(owner), cols(side)] + near[s, side, 0]
        for j in peers:
            to_peer(s, side, j).wait_recv()
            value = value + decode(far[s, side, j - 1], far_scale[s, side, j - 1])
        if side == 1:
            edge[s], edge_scale[s] = encode(value)
            pl.when(has_right)(lambda: to_right(s).start())
        else:
            out_ref[s] = value

    def add_edge(s):
        to_right(s).wait_recv()
        out_ref[s] += decode(edge_in[s], edge_in_scale[s])

    groups_all = probes // GROUP
    lax.fori_loop(0, 1, enter, 0)
    pass_on(1, 0)
    pl.when(has_right)(lambda: pass_on(1, 1))
    lax.fori_loop(1, groups_all, enter, 0)
    landed(1, 0)
    pl.when(has_right)(lambda: landed(1, 1))
    lax.fori_loop(0, groups_all, forward, 0)
    give(1)
    lax.fori_loop(0, 1, backward, 0)
    across(1)
    lax.fori_loop(1, groups_all, backward, 0)
    collect(1, 1)
    give(0)
    across(0)
    collect(1, 0)
    collect(0, 1)
    collect(0, 0)
    for s in (1, 0):
        pl.when(has_left)(lambda s=s: add_edge(s))

    for s in range(layers):
        sent(s, 0)
        pl.when(has_right)(lambda s=s: sent(s, 1))
        pl.when(has_left)(lambda s=s: g_left(s).wait_send())
        for side in (0, 1):
            for j in peers + [0]:
                to_partner(s, side, j).wait_send()
            for j in peers:
                to_peer(s, side, j).wait_send()
        pl.when(has_right)(lambda s=s: to_right(s).wait_send())


def fused(rows_part, positions, illumination, measured):
    owners = lax.axis_size("owner")
    layers, size, width = rows_part.shape
    probes = measured.shape[0]
    chips = owners // 2
    peers = max(chips - 1, 1)
    right, left = triple_tables(width)
    tile = lax.axis_index("tile")
    row = positions[:, 0] - tile // TX * (owners * size)
    col = positions[:, 1] - tile % TX * width
    base = jnp.minimum(row // ALIGN * ALIGN, owners * size - width - ALIGN)
    starts = size + jnp.arange(owners)[None, :] * size - (row // 8 * 8)[:, None]
    starts = jnp.clip(starts, 0, size + width + 8)
    heads = jnp.stack([base // ALIGN, row - base, col, row % 8], axis=1)
    place = jnp.concatenate([heads, starts // 8], axis=1)
    place = place.astype(jnp.int32)
    grouped = rows_part.reshape(layers, size // ALIGN, ALIGN, width)
    vmem = pl.BlockSpec(memory_space=pltpu.VMEM)
    anywhere = pl.BlockSpec(memory_space=pl.ANY)
    block = (size, width)
    f32 = jnp.float32
    flops = probes * 4 * 2 * 3 * 2 * (2 * width) ** 2 * width
    return pl.pallas_call(
        functools.partial(fused_kernel, owners),
        out_shape=jax.ShapeDtypeStruct((layers,) + block, f32),
        in_specs=[pl.BlockSpec(memory_space=pltpu.SMEM), vmem, vmem] + [anywhere] * 3,
        out_specs=vmem,
        scratch_shapes=[
            pltpu.VMEM((owners * size // ALIGN, ALIGN, 2 * width), rows_part.dtype),
            pltpu.VMEM((owners * size // ALIGN, ALIGN, 2 * width), rows_part.dtype),
            pltpu.VMEM(measured.shape, f32),
            pltpu.VMEM(right.shape, jnp.bfloat16),
            pltpu.VMEM(left.shape, jnp.bfloat16),
            pltpu.VMEM((probes, 2, width, width), f32),
            pltpu.VMEM((probes, 2, width, width), f32),
            pltpu.VMEM((probes, (2 * size + width) // 8 + 1, 8, 2 * width), f32),
            pltpu.VMEM((layers, owners * size, 2 * width), f32),
            pltpu.VMEM((layers, 2, chips) + block, f32),
            pltpu.VMEM((layers, 2, peers) + block, jnp.int16),
            pltpu.VMEM((layers, 2, peers) + block, jnp.int16),
            pltpu.VMEM((layers,) + block, jnp.int16),
            pltpu.VMEM((layers,) + block, jnp.int16),
            pltpu.VMEM((layers, 2, peers, 8, width), f32),
            pltpu.VMEM((layers, 2, peers, 8, width), f32),
            pltpu.VMEM((layers, 8, width), f32),
            pltpu.VMEM((layers, 8, width), f32),
            pltpu.SemaphoreType.DMA((3,)),
            pltpu.SemaphoreType.DMA((layers, 3 + 4 * (chips - 1))),
            pltpu.SemaphoreType.DMA((layers, 3 + 4 * (chips - 1))),
            pltpu.SemaphoreType.DMA((layers, 6 * chips - 2)),
            pltpu.SemaphoreType.DMA((layers, 6 * chips - 2)),
        ],
        compiler_params=pltpu.CompilerParams(
            collective_id=2, has_side_effects=True, vmem_limit_bytes=56 * 2**20
        ),
        cost_estimate=pl.CostEstimate(flops=flops, bytes_accessed=8 * 2**20, transcendentals=0),
    )(place, grouped, illumination, measured, right, left)


def body(potential, positions, illumination, measured):
    probe_width = illumination.shape[1]
    rows_part = potential[:, 0]
    layers = rows_part.shape[0]
    tile_rows = rows_part.shape[1] * lax.axis_size("owner")
    tile_cols = rows_part.shape[2]
    below = lax.axis_size("tile") > TX
    if not below and layers == 2 and measured.shape[0] % GROUP == 0:
        return fused(rows_part, positions, illumination, measured)[:, None]
    extended = gather_grid(rows_part)
    if below:
        lower_rim = passed_along(extended[:, :probe_width, :], "tile", -TX)
        extended = jnp.concatenate([extended, lower_rim], axis=1)
    tile_id = lax.axis_index("tile")
    first = jnp.stack([tile_id // TX * tile_rows, tile_id % TX * tile_cols])
    corners = positions - first[None, :].astype(jnp.int32)
    accumulated = probe_gradients(corners, extended, illumination, measured)
    wide_grad = accumulated[:, :tile_rows, :]
    if below:
        upper_back = passed_along(accumulated[:, tile_rows:, :], "tile", TX)
        wide_grad = wide_grad.at[:, :probe_width, :].add(upper_back)
    return reduce_grid(wide_grad)[:, None]


def solution(mesh):
    in_specs = (
        P(None, "tile", "owner", None),
        P(("tile", "owner"), None),
        P(),
        P(("tile", "owner"), None, None),
    )
    out_specs = P(None, "tile", "owner", None)
    return jax.shard_map(body, mesh=mesh, in_specs=in_specs, out_specs=out_specs, check_vma=False)
```

```python
import functools
import math

import jax
import jax.numpy as jnp
import numpy as np
from jax import lax
from jax.experimental import pallas as pl
from jax.experimental.pallas import tpu as pltpu
from jax.sharding import PartitionSpec as P

TX = 8

SIGMA = 0.5
LOSS_WEIGHT = 0.125
ALIGN = 16
GROUP = 2
MESH = pl.DeviceIdType.MESH


def passed_along(block, axis, distance):
    devices = range(lax.axis_size(axis))
    route = [(i - distance, i) for i in devices if i - distance in devices]
    return lax.ppermute(block, axis, route)


def block_tables(width):
    counter = np.arange(width)
    signed = (counter + width // 2) % width - width // 2
    angle = 2.0 * np.pi / width * (counter[:, None] * counter[None, :] % width)
    dft = np.exp(-1j * angle) / math.sqrt(width)
    chirp = np.exp(-4j * np.pi * signed.astype(np.float64) ** 2 / (width * width))
    prop = (np.conj(dft) * chirp[None, :]) @ dft

    def right(m):
        return np.block([[m.real, m.imag], [-m.imag, m.real]])

    full = np.stack([right(dft), right(np.conj(dft)), right(prop), right(np.conj(prop))])
    full = full.astype(np.float32)
    high = full.astype(jnp.bfloat16)
    low = (full - high.astype(np.float32)).astype(jnp.bfloat16)
    return high, low


def halves(x):
    high = x.astype(jnp.bfloat16)
    low = (x - high.astype(jnp.float32)).astype(jnp.bfloat16)
    return high, low


def dot3(a, b):
    def dot(x, y):
        return jnp.dot(x, y, preferred_element_type=jnp.float32)

    return dot(a[0], b[0]) + (dot(a[0], b[1]) + dot(a[1], b[0]))


def both_sides(real, imag, high, low, which):
    width = real.shape[0]
    wide = jnp.concatenate([real, imag], axis=1)
    wide = dot3(halves(wide), (high[which], low[which]))
    tall = jnp.concatenate([wide[:, :width], wide[:, width:]], axis=0)
    other = which ^ 1
    tall = dot3((high[other], low[other]), halves(tall))
    return tall[:width], tall[width:]


def triple_tables(width):
    high, low = block_tables(width)
    right = np.concatenate([high, high, low], axis=1)
    left = np.concatenate([high, low, high], axis=2)
    return jnp.asarray(right), jnp.asarray(left)


def both_sides_of(waves, right, left, which):
    width = waves[0][0].shape[0]

    def dot(x, y):
        return jnp.dot(x, y, preferred_element_type=jnp.float32)

    wide = jnp.concatenate([jnp.concatenate(wave, axis=1) for wave in waves], axis=0)
    a, b = halves(wide)
    wide = dot(jnp.concatenate([a, b, a], axis=1), right[which])
    spans = [slice(k * width, (k + 1) * width) for k in range(len(waves))]
    real = jnp.concatenate([wide[span, :width] for span in spans], axis=1)
    imag = jnp.concatenate([wide[span, width:] for span in spans], axis=1)
    a, b = halves(jnp.concatenate([real, imag], axis=0))
    tall = dot(left[which ^ 1], jnp.concatenate([a, a, b], axis=0))
    return [(tall[:width, span], tall[width:, span]) for span in spans]


def turn(window):
    y = (0.5 * SIGMA) * window
    z = y * y
    sine = -1.0 / 39916800.0
    for c in (1.0 / 362880.0, -1.0 / 5040.0, 1.0 / 120.0, -1.0 / 6.0, 1.0):
        sine = sine * z + c
    sine = sine * y
    cosine = 1.0 / 479001600.0
    for c in (-1.0 / 3628800.0, 1.0 / 40320.0, -1.0 / 720.0, 1.0 / 24.0, -0.5, 1.0):
        cosine = cosine * z + c
    return 1.0 - 2.0 * sine * sine, 2.0 * sine * cosine


def probes_kernel(corner_ref, ext_ref, illum_ref, meas_ref, high, low, acc_ref):
    width = illum_ref.shape[1]
    rows, cols = ext_ref.shape[1], ext_ref.shape[2]
    span = width + ALIGN
    acc_ref[...] = jnp.zeros_like(acc_ref)

    def probe(p, carry):
        r = corner_ref[p, 0]
        c = corner_ref[p, 1]
        base = pl.multiple_of(jnp.minimum((r // ALIGN) * ALIGN, rows - span), ALIGN)
        shift = r - base

        def cut(s):
            x = ext_ref[s, pl.ds(base, span), :].astype(jnp.float32)
            x = pltpu.roll(x, span - shift, 0)[:width]
            return pltpu.roll(x, cols - c, 1)[:, :width]

        def paste(s, g):
            x = jnp.concatenate([g, jnp.zeros((width, cols - width), jnp.float32)], axis=1)
            x = pltpu.roll(x, c, 1)
            x = jnp.concatenate([x, jnp.zeros((ALIGN, cols), jnp.float32)], axis=0)
            acc_ref[s, pl.ds(base, span), :] += pltpu.roll(x, shift, 0)

        cos0, sin0 = turn(cut(0))
        first_r = illum_ref[0] * cos0 - illum_ref[1] * sin0
        first_i = illum_ref[0] * sin0 + illum_ref[1] * cos0
        mid_r, mid_i = both_sides(first_r, first_i, high, low, 2)
        cos1, sin1 = turn(cut(1))
        exit_r = mid_r * cos1 - mid_i * sin1
        exit_i = mid_r * sin1 + mid_i * cos1
        far_r, far_i = both_sides(exit_r, exit_i, high, low, 0)
        misfit = far_r * far_r + far_i * far_i - meas_ref[p]
        scale = (4.0 * LOSS_WEIGHT) * misfit
        g_r, g_i = both_sides(scale * far_r, scale * far_i, high, low, 1)
        paste(1, SIGMA * (g_i * exit_r - g_r * exit_i))
        b_r = g_r * cos1 + g_i * sin1
        b_i = g_i * cos1 - g_r * sin1
        g_r, g_i = both_sides(b_r, b_i, high, low, 3)
        paste(0, SIGMA * (g_i * first_r - g_r * first_i))
        return carry

    lax.fori_loop(0, meas_ref.shape[0], probe, 0)


def probe_gradients(corners, extended, illumination, measured, interpret=False):
    high, low = block_tables(illumination.shape[1])
    vmem = pl.BlockSpec(memory_space=pltpu.VMEM)
    probes, width = measured.shape[0], measured.shape[1]
    flops = probes * 4 * 2 * 3 * 2 * (2 * width) ** 2 * width
    return pl.pallas_call(
        probes_kernel,
        out_shape=jax.ShapeDtypeStruct(extended.shape, jnp.float32),
        in_specs=[pl.BlockSpec(memory_space=pltpu.SMEM)] + [vmem] * 5,
        out_specs=vmem,
        compiler_params=pltpu.CompilerParams(vmem_limit_bytes=56 * 2**20),
        cost_estimate=pl.CostEstimate(flops=flops, bytes_accessed=16 * 2**20, transcendentals=0),
        interpret=interpret,
    )(corners, extended, illumination, measured, jnp.asarray(high), jnp.asarray(low))


def places():
    tile, owner = lax.axis_index("tile"), lax.axis_index("owner")
    partner = owner + 1 - 2 * (owner % 2)
    return tile, owner, partner, tile % TX != 0, tile % TX != TX - 1


def greet(owners):
    tile, owner, partner, has_left, has_right = places()
    barrier = pltpu.get_barrier_semaphore()

    def hello(device):
        pl.semaphore_signal(barrier, inc=1, device_id=device, device_id_type=MESH)

    hello({"owner": partner})
    for j in range(1, owners // 2):
        hello({"owner": (owner + 2 * j) % owners})
    pl.when(has_left)(lambda: hello({"tile": tile - 1}))
    pl.when(has_right)(lambda: hello({"tile": tile + 1}))
    beside = has_left.astype(jnp.int32) + has_right.astype(jnp.int32)
    pl.semaphore_wait(barrier, owners // 2 + beside)


def gather_kernel(owners, part_ref, ext_ref, send, recv):
    tile, owner, partner, has_left, has_right = places()
    layers, size, width = part_ref.shape
    chips = owners // 2
    peers = range(1, chips)

    def spot(s, who, side):
        start = pl.multiple_of(who * size, size)
        return ext_ref.at[s, pl.ds(start, size), pl.ds(side * width, width)]

    def copy(s, kind, src, dst, device):
        return pltpu.make_async_remote_copy(
            src_ref=src, dst_ref=dst, send_sem=send.at[s, kind], recv_sem=recv.at[s, kind],
            device_id=device, device_id_type=MESH,
        )

    def to_left(s):
        return copy(s, 0, part_ref.at[s], spot(s, owner, 1), {"tile": tile - 1})

    def to_partner(s, side):
        src = part_ref.at[s] if side == 0 else spot(s, owner, 1)
        return copy(s, 1 + side, src, spot(s, owner, side), {"owner": partner})

    def to_peer(s, side, j):
        src = part_ref.at[s] if side == 0 else spot(s, owner, 1)
        kind = 3 + side * (chips - 1) + j - 1
        return copy(s, kind, src, spot(s, owner, side), {"owner": (owner + 2 * j) % owners})

    def onward(s, side, j):
        block = spot(s, (owner + owners - 2 * j) % owners, side)
        kind = 3 + (2 + side) * (chips - 1) + j - 1
        return copy(s, kind, block, block, {"owner": partner})

    greet(owners)

    def spread(s, side):
        for j in peers:
            to_peer(s, side, j).start()
        to_partner(s, side).start()

    def pass_on(s, side):
        for j in peers:
            to_peer(s, side, j).wait_recv()
            onward(s, side, j).start()

    def finish(s, side):
        to_partner(s, side).wait()
        for j in peers:
            to_peer(s, side, j).wait_send()
            onward(s, side, j).wait()

    for s in range(layers):
        pl.when(has_left)(lambda s=s: to_left(s).start())
    spread(0, 0)
    for s in range(layers):
        @pl.when(has_right)
        def _(s=s):
            to_left(s).wait_recv()
            spread(s, 1)

        if s + 1 < layers:
            spread(s + 1, 0)
        ext_ref[s, pl.ds(pl.multiple_of(owner * size, size), size), :width] = part_ref[s]

        @pl.when(jnp.logical_not(has_right))
        def _(s=s):
            ext_ref[s, :, width:] = jnp.zeros((ext_ref.shape[1], width), ext_ref.dtype)

    for s in range(layers):
        pass_on(s, 0)
        pl.when(has_right)(lambda s=s: pass_on(s, 1))
    for s in range(layers):
        finish(s, 0)
        pl.when(has_right)(lambda s=s: finish(s, 1))
        pl.when(has_left)(lambda s=s: to_left(s).wait_send())


def gather_grid(rows_part):
    owners = lax.axis_size("owner")
    layers, size, width = rows_part.shape
    kinds = 3 + 4 * (owners // 2 - 1)
    vmem = pl.BlockSpec(memory_space=pltpu.VMEM)
    return pl.pallas_call(
        functools.partial(gather_kernel, owners),
        out_shape=jax.ShapeDtypeStruct((layers, owners * size, 2 * width), rows_part.dtype),
        in_specs=[vmem],
        out_specs=vmem,
        scratch_shapes=[pltpu.SemaphoreType.DMA((layers, kinds))] * 2,
        compiler_params=pltpu.CompilerParams(
            collective_id=0, has_side_effects=True, vmem_limit_bytes=56 * 2**20
        ),
    )(rows_part)


def reduce_kernel(owners, grad_ref, out_ref, near, total, far, edge, edge_in, sends, recvs):
    tile, owner, partner, has_left, has_right = places()
    layers, size, width = out_ref.shape
    chips = owners // 2
    order = [(s, side) for side in (1, 0) for s in range(layers)]

    def rows(who):
        return pl.ds(pl.multiple_of(who * size, size), size)

    def cols(side):
        return pl.ds(side * width, width)

    def to_partner(s, side, j):
        src = grad_ref.at[s, rows((partner + 2 * j) % owners), cols(side)]
        return pltpu.make_async_remote_copy(
            src_ref=src, dst_ref=near.at[s, side, j],
            send_sem=sends.at[s, side, j], recv_sem=recvs.at[s, side, j],
            device_id={"owner": partner}, device_id_type=MESH,
        )

    def to_peer(s, side, j):
        return pltpu.make_async_remote_copy(
            src_ref=total.at[s, side, j - 1], dst_ref=far.at[s, side, j - 1],
            send_sem=sends.at[s, side, chips + j - 1], recv_sem=recvs.at[s, side, chips + j - 1],
            device_id={"owner": (owner + 2 * j) % owners}, device_id_type=MESH,
        )

    def to_right(s):
        return pltpu.make_async_remote_copy(
            src_ref=edge.at[s], dst_ref=edge_in.at[s],
            send_sem=sends.at[s, 0, 2 * chips - 1], recv_sem=recvs.at[s, 0, 2 * chips - 1],
            device_id={"tile": tile + 1}, device_id_type=MESH,
        )

    greet(owners)
    peers = list(range(1, chips))
    for s, side in order:
        for j in peers + [0]:
            to_partner(s, side, j).start()
    for s, side in order:
        for j in peers:
            to_partner(s, side, j).wait_recv()
            own = grad_ref[s, rows((owner + 2 * j) % owners), cols(side)]
            total[s, side, j - 1] = own + near[s, side, j]
            to_peer(s, side, j).start()
    for s, side in order:
        to_partner(s, side, 0).wait_recv()
        value = grad_ref[s, rows(owner), cols(side)] + near[s, side, 0]
        for j in peers:
            to_peer(s, side, j).wait_recv()
            value = value + far[s, side, j - 1]
        if side == 1:
            edge[s] = value
            pl.when(has_right)(lambda s=s: to_right(s).start())
        else:
            out_ref[s] = value
    for s in range(layers):
        @pl.when(has_left)
        def _(s=s):
            to_right(s).wait_recv()
            out_ref[s] += edge_in[s]

    for s, side in order:
        for j in peers + [0]:
            to_partner(s, side, j).wait_send()
        for j in peers:
            to_peer(s, side, j).wait_send()
    for s in range(layers):
        pl.when(has_right)(lambda s=s: to_right(s).wait_send())


def reduce_grid(wide_grad):
    owners = lax.axis_size("owner")
    layers, tile_rows, cols = wide_grad.shape
    size, width, chips = tile_rows // owners, cols // 2, owners // 2
    vmem = pl.BlockSpec(memory_space=pltpu.VMEM)
    block = (size, width)
    return pl.pallas_call(
        functools.partial(reduce_kernel, owners),
        out_shape=jax.ShapeDtypeStruct((layers,) + block, jnp.float32),
        in_specs=[vmem],
        out_specs=vmem,
        scratch_shapes=[
            pltpu.VMEM((layers, 2, chips) + block, jnp.float32),
            pltpu.VMEM((layers, 2, max(chips - 1, 1)) + block, jnp.float32),
            pltpu.VMEM((layers, 2, max(chips - 1, 1)) + block, jnp.float32),
            pltpu.VMEM((layers,) + block, jnp.float32),
            pltpu.VMEM((layers,) + block, jnp.float32),
            pltpu.SemaphoreType.DMA((layers, 2, 2 * chips)),
            pltpu.SemaphoreType.DMA((layers, 2, 2 * chips)),
        ],
        compiler_params=pltpu.CompilerParams(
            collective_id=1, has_side_effects=True, vmem_limit_bytes=56 * 2**20
        ),
    )(wide_grad)


def encode(x):
    largest = jnp.maximum(jnp.max(jnp.abs(x), axis=0, keepdims=True), 1e-30)
    code = jnp.round(x * (32767.0 / largest)).astype(jnp.int32).astype(jnp.int16)
    return code, jnp.broadcast_to(largest * (1.0 / 32767.0), (8, x.shape[1]))


def decode(code, scale):
    return code.astype(jnp.int32).astype(jnp.float32) * scale[:1]


class Several:
    def __init__(self, *copies):
        self.copies = copies

    def start(self):
        for copy in self.copies:
            copy.start()

    def wait_send(self):
        for copy in self.copies:
            copy.wait_send()

    def wait_recv(self):
        for copy in self.copies:
            copy.wait_recv()


def fused_kernel(
    owners, place_ref, part_ref, illum_ref, meas_hbm, right_hbm, left_hbm, out_ref,
    ext0, ext1, meas_ref, right, left, first, back, pads, grad, near, total, far, edge, edge_in,
    total_scale, far_scale, edge_scale, edge_in_scale, loads, g_send, g_recv, sends, recvs,
):
    tile, owner, partner, has_left, has_right = places()
    layers, groups, _, width = part_ref.shape
    size = groups * ALIGN
    chips = owners // 2
    peers = list(range(1, chips))
    probes = meas_ref.shape[0]
    cols_all = 2 * width
    rows_all = owners * size
    span = width + ALIGN
    ext = (ext0, ext1)
    tail = width + 8

    fetches = [
        pltpu.make_async_copy(src, dst, loads.at[i])
        for i, (src, dst) in enumerate(((right_hbm, right), (left_hbm, left), (meas_hbm, meas_ref)))
    ]
    for fetch in fetches:
        fetch.start()
    greet(owners)

    def spot(s, who, side):
        return ext[s].at[pl.ds(who * groups, groups), :, pl.ds(side * width, width)]

    def g_copy(s, kind, src, dst, device):
        return pltpu.make_async_remote_copy(
            src_ref=src, dst_ref=dst, send_sem=g_send.at[s, kind], recv_sem=g_recv.at[s, kind],
            device_id=device, device_id_type=MESH,
        )

    def own(s, side):
        return part_ref.at[s] if side == 0 else spot(s, owner, 1)

    def g_left(s):
        return g_copy(s, 0, part_ref.at[s], spot(s, owner, 1), {"tile": tile - 1})

    def g_partner(s, side):
        return g_copy(s, 1 + side, own(s, side), spot(s, owner, side), {"owner": partner})

    def g_peer(s, side, j):
        kind = 3 + side * (chips - 1) + j - 1
        device = {"owner": (owner + 2 * j) % owners}
        return g_copy(s, kind, own(s, side), spot(s, owner, side), device)

    def g_onward(s, side, j):
        block = spot(s, (owner + owners - 2 * j) % owners, side)
        kind = 3 + (2 + side) * (chips - 1) + j - 1
        return g_copy(s, kind, block, block, {"owner": partner})

    def spread(s, side):
        for j in peers:
            g_peer(s, side, j).start()
        g_partner(s, side).start()

    def pass_on(s, side):
        for j in peers:
            g_peer(s, side, j).wait_recv()
            g_onward(s, side, j).start()

    def landed(s, side):
        g_partner(s, side).wait_recv()
        for j in peers:
            g_onward(s, side, j).wait_recv()

    def sent(s, side):
        g_partner(s, side).wait_send()
        for j in peers:
            g_peer(s, side, j).wait_send()
            g_onward(s, side, j).wait_send()

    def right_spread(s):
        g_left(s).wait_recv()
        spread(s, 1)

    pl.when(has_left)(lambda: g_left(0).start())
    spread(0, 0)
    blank = jnp.zeros((probes, size // 8, 8, cols_all), jnp.float32)
    pads[:, : size // 8] = blank
    pads[:, (size + tail) // 8 :] = blank
    for s in range(layers):
        ext[s][pl.ds(owner * groups, groups), :, :width] = part_ref[s]

        @pl.when(jnp.logical_not(has_right))
        def _(s=s):
            ext[s][:, :, width:] = jnp.zeros((rows_all // ALIGN, ALIGN, width), part_ref.dtype)

    pl.when(has_right)(lambda: right_spread(0))
    pl.when(has_left)(lambda: g_left(1).start())
    spread(1, 0)
    pass_on(0, 0)
    pl.when(has_right)(lambda: pass_on(0, 1))
    landed(0, 0)
    pl.when(has_right)(lambda: landed(0, 1))
    pl.when(has_right)(lambda: right_spread(1))
    for fetch in fetches:
        fetch.wait()

    def pick(shape, dim, shift):
        along = lax.broadcasted_iota(jnp.int32, shape, dim)
        other = lax.broadcasted_iota(jnp.int32, shape, 1 - dim)
        return jnp.where(along == other + shift, 1.0, 0.0).astype(jnp.bfloat16)

    def dot(x, y):
        return jnp.dot(x, y, preferred_element_type=jnp.float32)

    def cut(s, p):
        base = place_ref[p, 0]
        x = jnp.concatenate([ext[s][base + i] for i in range(span // ALIGN)], axis=0)
        x = dot(x, pick((cols_all, width), 0, place_ref[p, 2])).astype(jnp.bfloat16)
        return dot(pick((width, span), 1, place_ref[p, 1]), x)

    def paste(p, g):
        down = pick((tail, width), 0, place_ref[p, 3])
        a, b = halves(g)
        a, b = halves(dot(down, a) + dot(down, b))
        along = pick((width, cols_all), 1, place_ref[p, 2])
        value = dot(a, along) + dot(b, along)
        pads[p, pl.ds(size // 8, tail // 8)] = value.reshape(tail // 8, 8, cols_all)

    def members(g):
        return [g * GROUP + k for k in range(GROUP)]

    def enter(g, carry):
        waves = []
        for p in members(g):
            cos0, sin0 = turn(cut(0, p))
            first[p, 0] = illum_ref[0] * cos0 - illum_ref[1] * sin0
            first[p, 1] = illum_ref[0] * sin0 + illum_ref[1] * cos0
            waves.append((first[p, 0], first[p, 1]))
        waves = both_sides_of(waves, right, left, 2)
        for p, (real, imag) in zip(members(g), waves):
            back[p, 0] = real
            back[p, 1] = imag
        return carry

    def forward(g, carry):
        turns, exits = [], []
        for p in members(g):
            cos1, sin1 = turn(cut(1, p))
            mid_r, mid_i = back[p, 0], back[p, 1]
            turns.append((cos1, sin1))
            exits.append((mid_r * cos1 - mid_i * sin1, mid_r * sin1 + mid_i * cos1))
        waves = []
        for p, (far_r, far_i) in zip(members(g), both_sides_of(exits, right, left, 0)):
            misfit = far_r * far_r + far_i * far_i - meas_ref[p]
            scale = (4.0 * LOSS_WEIGHT) * misfit
            waves.append((scale * far_r, scale * far_i))
        waves = both_sides_of(waves, right, left, 1)
        for p, (g_r, g_i), (cos1, sin1), (exit_r, exit_i) in zip(members(g), waves, turns, exits):
            back[p, 0] = g_r * cos1 + g_i * sin1
            back[p, 1] = g_i * cos1 - g_r * sin1
            paste(p, SIGMA * (g_i * exit_r - g_r * exit_i))
        return carry

    def backward(g, carry):
        waves = both_sides_of([(back[p, 0], back[p, 1]) for p in members(g)], right, left, 3)
        for p, (g_r, g_i) in zip(members(g), waves):
            paste(p, SIGMA * (g_i * first[p, 0] - g_r * first[p, 1]))
        return carry

    part = width // 2
    right_sides, left_sides = (3, 2), (1, 0)

    def rows(who):
        return pl.ds(pl.multiple_of(who * size, size), size)

    def cols(side):
        return pl.ds(side * part, part)

    def r_copy(s, kind, src, dst, device):
        return pltpu.make_async_remote_copy(
            src_ref=src, dst_ref=dst, send_sem=sends.at[s, kind], recv_sem=recvs.at[s, kind],
            device_id=device, device_id_type=MESH,
        )

    def to_partner(s, side, j):
        src = grad.at[s, rows((partner + 2 * j) % owners), cols(side)]
        return r_copy(s, side * chips + j, src, near.at[s, side, j], {"owner": partner})

    def to_peer(s, side, j):
        kind = 4 * chips + side * (chips - 1) + j - 1
        device = {"owner": (owner + 2 * j) % owners}
        at = (s, side, j - 1)
        more = kind + 4 * (chips - 1)
        return Several(
            r_copy(s, kind, total.at[at], far.at[at], device),
            r_copy(s, more, total_scale.at[at], far_scale.at[at], device),
        )

    def to_right(s, side):
        kind = 12 * chips - 8 + 2 * (side - 2)
        device = {"tile": tile + 1}
        return Several(
            r_copy(s, kind, edge.at[s, side - 2], edge_in.at[s, side - 2], device),
            r_copy(s, kind + 1, edge_scale.at[s, side - 2], edge_in_scale.at[s, side - 2], device),
        )

    def block_sum(who, side):
        starts = [place_ref[p, 4 + who] for p in range(probes)]
        parts = []
        for i in range(size // 8):
            terms = [pads[p, starts[p] + i, :, cols(side)] for p in range(probes)]
            parts.append(functools.reduce(jnp.add, terms))
        value = jnp.concatenate(parts, axis=0)
        return value

    def give(s):
        for side in right_sides + left_sides:
            for j in peers + [0]:
                who = (partner + 2 * j) % owners
                grad[s, rows(who), cols(side)] = block_sum(who, side)
                to_partner(s, side, j).start()
        for side in right_sides + left_sides:
            for j in peers + [0]:
                who = (owner + 2 * j) % owners
                grad[s, rows(who), cols(side)] = block_sum(who, side)

    def across(s):
        for side in right_sides + left_sides:
            for j in peers:
                to_partner(s, side, j).wait_recv()
                mine = grad[s, rows((owner + 2 * j) % owners), cols(side)]
                code, scale = encode(mine + near[s, side, j])
                total[s, side, j - 1] = code
                total_scale[s, side, j - 1] = scale
                to_peer(s, side, j).start()

    def collect(s, side):
        to_partner(s, side, 0).wait_recv()
        value = grad[s, rows(owner), cols(side)] + near[s, side, 0]
        for j in peers:
            to_peer(s, side, j).wait_recv()
            value = value + decode(far[s, side, j - 1], far_scale[s, side, j - 1])
        if side in right_sides:
            edge[s, side - 2], edge_scale[s, side - 2] = encode(value)
            pl.when(has_right)(lambda: to_right(s, side).start())
        else:
            out_ref[s, :, cols(side)] = value

    def add_edge(s):
        for side in right_sides:
            to_right(s, side).wait_recv()
            add = decode(edge_in[s, side - 2], edge_in_scale[s, side - 2])
            out_ref[s, :, cols(side - 2)] += add

    groups_all = probes // GROUP
    lax.fori_loop(0, 1, enter, 0)
    pass_on(1, 0)
    pl.when(has_right)(lambda: pass_on(1, 1))
    lax.fori_loop(1, groups_all, enter, 0)
    landed(1, 0)
    pl.when(has_right)(lambda: landed(1, 1))
    lax.fori_loop(0, groups_all, forward, 0)
    give(1)
    lax.fori_loop(0, 1, backward, 0)
    across(1)
    lax.fori_loop(1, groups_all, backward, 0)
    for side in right_sides:
        collect(1, side)
    give(0)
    across(0)
    for side in left_sides:
        collect(1, side)
    for side in right_sides + left_sides:
        collect(0, side)
    for s in (1, 0):
        pl.when(has_left)(lambda s=s: add_edge(s))

    for s in range(layers):
        sent(s, 0)
        pl.when(has_right)(lambda s=s: sent(s, 1))
        pl.when(has_left)(lambda s=s: g_left(s).wait_send())
        for side in right_sides + left_sides:
            for j in peers + [0]:
                to_partner(s, side, j).wait_send()
            for j in peers:
                to_peer(s, side, j).wait_send()
        for side in right_sides:
            pl.when(has_right)(lambda s=s, side=side: to_right(s, side).wait_send())


def fused(rows_part, positions, illumination, measured):
    owners = lax.axis_size("owner")
    layers, size, width = rows_part.shape
    probes = measured.shape[0]
    chips = owners // 2
    peers = max(chips - 1, 1)
    right, left = triple_tables(width)
    tile = lax.axis_index("tile")
    row = positions[:, 0] - tile // TX * (owners * size)
    col = positions[:, 1] - tile % TX * width
    base = jnp.minimum(row // ALIGN * ALIGN, owners * size - width - ALIGN)
    starts = size + jnp.arange(owners)[None, :] * size - (row // 8 * 8)[:, None]
    starts = jnp.clip(starts, 0, size + width + 8)
    heads = jnp.stack([base // ALIGN, row - base, col, row % 8], axis=1)
    place = jnp.concatenate([heads, starts // 8], axis=1)
    place = place.astype(jnp.int32)
    grouped = rows_part.reshape(layers, size // ALIGN, ALIGN, width)
    vmem = pl.BlockSpec(memory_space=pltpu.VMEM)
    anywhere = pl.BlockSpec(memory_space=pl.ANY)
    block = (size, width)
    chunk = (size, width // 2)
    f32 = jnp.float32
    flops = probes * 4 * 2 * 3 * 2 * (2 * width) ** 2 * width
    return pl.pallas_call(
        functools.partial(fused_kernel, owners),
        out_shape=jax.ShapeDtypeStruct((layers,) + block, f32),
        in_specs=[pl.BlockSpec(memory_space=pltpu.SMEM), vmem, vmem] + [anywhere] * 3,
        out_specs=vmem,
        scratch_shapes=[
            pltpu.VMEM((owners * size // ALIGN, ALIGN, 2 * width), rows_part.dtype),
            pltpu.VMEM((owners * size // ALIGN, ALIGN, 2 * width), rows_part.dtype),
            pltpu.VMEM(measured.shape, f32),
            pltpu.VMEM(right.shape, jnp.bfloat16),
            pltpu.VMEM(left.shape, jnp.bfloat16),
            pltpu.VMEM((probes, 2, width, width), f32),
            pltpu.VMEM((probes, 2, width, width), f32),
            pltpu.VMEM((probes, (2 * size + width) // 8 + 1, 8, 2 * width), f32),
            pltpu.VMEM((layers, owners * size, 2 * width), f32),
            pltpu.VMEM((layers, 4, chips) + chunk, f32),
            pltpu.VMEM((layers, 4, peers) + chunk, jnp.int16),
            pltpu.VMEM((layers, 4, peers) + chunk, jnp.int16),
            pltpu.VMEM((layers, 2) + chunk, jnp.int16),
            pltpu.VMEM((layers, 2) + chunk, jnp.int16),
            pltpu.VMEM((layers, 4, peers, 8, width // 2), f32),
            pltpu.VMEM((layers, 4, peers, 8, width // 2), f32),
            pltpu.VMEM((layers, 2, 8, width // 2), f32),
            pltpu.VMEM((layers, 2, 8, width // 2), f32),
            pltpu.SemaphoreType.DMA((3,)),
            pltpu.SemaphoreType.DMA((layers, 3 + 4 * (chips - 1))),
            pltpu.SemaphoreType.DMA((layers, 3 + 4 * (chips - 1))),
            pltpu.SemaphoreType.DMA((layers, 12 * chips - 4)),
            pltpu.SemaphoreType.DMA((layers, 12 * chips - 4)),
        ],
        compiler_params=pltpu.CompilerParams(
            collective_id=2, has_side_effects=True, vmem_limit_bytes=56 * 2**20
        ),
        cost_estimate=pl.CostEstimate(flops=flops, bytes_accessed=8 * 2**20, transcendentals=0),
    )(place, grouped, illumination, measured, right, left)


def body(potential, positions, illumination, measured):
    probe_width = illumination.shape[1]
    rows_part = potential[:, 0]
    layers = rows_part.shape[0]
    tile_rows = rows_part.shape[1] * lax.axis_size("owner")
    tile_cols = rows_part.shape[2]
    below = lax.axis_size("tile") > TX
    if not below and layers == 2 and measured.shape[0] % GROUP == 0:
        return fused(rows_part, positions, illumination, measured)[:, None]
    extended = gather_grid(rows_part)
    if below:
        lower_rim = passed_along(extended[:, :probe_width, :], "tile", -TX)
        extended = jnp.concatenate([extended, lower_rim], axis=1)
    tile_id = lax.axis_index("tile")
    first = jnp.stack([tile_id // TX * tile_rows, tile_id % TX * tile_cols])
    corners = positions - first[None, :].astype(jnp.int32)
    accumulated = probe_gradients(corners, extended, illumination, measured)
    wide_grad = accumulated[:, :tile_rows, :]
    if below:
        upper_back = passed_along(accumulated[:, tile_rows:, :], "tile", TX)
        wide_grad = wide_grad.at[:, :probe_width, :].add(upper_back)
    return reduce_grid(wide_grad)[:, None]


def solution(mesh):
    in_specs = (
        P(None, "tile", "owner", None),
        P(("tile", "owner"), None),
        P(),
        P(("tile", "owner"), None, None),
    )
    out_specs = P(None, "tile", "owner", None)
    return jax.shard_map(body, mesh=mesh, in_specs=in_specs, out_specs=out_specs, check_vma=False)
```
